32 devices in a mesh: blk: 8 (over y, x, core), grp: 4 (over z).
Axes of the slice: x: 2, y: 2, z: 4, core: 2. Of those that a mesh axis runs over, the one named last changes fastest.
Arguments:
- raw_panels: bfloat16 [4, 1024, 8192], P('grp', 'blk'), may hold values from -0.4375 to 0.4375
- metric: bfloat16 [1024, 1024], replicated, may hold values from -0.1875 to 0.1875
- tile_pairs: int32 [112, 2], P('blk'), may hold values from 0 to 7, as said below
- owners: int32 [112, 1], P('blk'), may hold values from 0 to 7; in each aligned block of 14 rows (0 to 13, 14 to 27, ...) at most 3 rows name the same one
- group_mask: int32 [112, 4], P('blk', 'grp'), may hold values 0 or 1
Outputs:
- owned_tiles: float32 [8, 8, 3, 128, 128], P('blk', None, None, 'grp')
The draws below stay inside these ranges and needn't reach their ends.
Inputs may be any that keep to these rules, and one draw needn't show every extreme that they name: `tile_pairs`: tile rows of source s (rows s * 14 to s * 14 + 13) have first entry s, the basis block held by index s of blk; the second entry differs from the first. `owners`: in each aligned block of 14 rows (one source) no owner appears more than 3 times.
All inputs are finite; a program needn't handle non-finite values. No bound on the sum of `group_mask` on one device may be relied on, other than what follows from the above.
Results may differ from the reference program's by a relative error of at most 0.0029.
Values may be sent and summed in bfloat16 or wider, within the bound.
No kernel may reach another device: no remote copies, remote signals or barrier semaphores. Data moves between devices by JAX's collectives and lax.ppermute only.
A program may use at most 128 MiB of HBM per device.

```python
import math
import jax
import jax.numpy as jnp
import numpy as np
from jax import lax

NAUX = 1024
OCC = 8
TILE = 128
TILE_DEV = 14
GROUPS = 4
NBAS = 1024
LOCAL = 1
NBLOCKS = 8
NTILE = 112
CAP = 3
N_BLK = 8


def draw_tile_pairs(key, part):
    key_local = jax.random.fold_in(key, 11)
    key_step = jax.random.fold_in(key, 23)
    device_of = jnp.arange(NTILE) // TILE_DEV
    local = jax.random.randint(key_local, (NTILE,), 0, LOCAL)
    first = device_of * LOCAL + local
    step = jax.random.randint(key_step, (NTILE,), 1, NBLOCKS)
    second = (first + step) % NBLOCKS
    return jnp.stack([first, second], axis=1).astype(jnp.int32)


def plant(array, key, smallest, largest):
    spot = [jax.random.randint(jax.random.fold_in(key, axis), (), 0, length) for axis, length in enumerate(array.shape)]
    longest = array.shape.index(max(array.shape))
    beside = spot[:longest] + [(spot[longest] + 1) % array.shape[longest]] + spot[longest + 1:]
    return array.at[tuple(spot)].set(smallest).at[tuple(beside)].set(largest)


def shard_levels(own_key, extent, cuts, low, top_value):
    gain, own = 1.0, jax.random.fold_in(own_key, 6)
    for axis_at, shards_of in cuts:
        heights = jnp.exp(jax.random.uniform(jax.random.fold_in(own, axis_at), (shards_of,), jnp.float32, low / len(cuts), top_value / len(cuts)))
        gain = gain * jnp.repeat(heights, extent[axis_at] // shards_of).reshape([-1 if axis == axis_at else 1 for axis in range(len(extent))])
    return gain


def assign_block(key, own, number, rows, count, top, most, skew):
    order = jax.random.permutation(key, count)
    crowded, ordinary = portions_of(count, rows * top, most, skew, True), portions_of(count, rows * top, most, skew, False)
    places = jnp.arange(count)

    def named(tallies, rotation):
        used = int((tallies > 0).sum())
        fixed = max(1, used // 4)
        moved = fixed + (places - fixed + rotation * (used - fixed)) % max(1, count - fixed)
        return jnp.zeros((count,), jnp.int32).at[order[jnp.where(places < fixed, places, moved)]].set(jnp.asarray(tallies, jnp.int32))

    tallies = jnp.where(number % 4 == 0, named(crowded, number // 4), named(ordinary, number - number // 4 - 1))
    mixed = jax.random.permutation(jax.random.fold_in(own, 3), count)
    source_of, receiver = mixed[0:count // 2 * 2:2], mixed[1:count // 2 * 2:2]
    room = jnp.minimum(tallies[source_of] - 1, most - tallies[receiver]) // 2
    room = jnp.where((source_of == order[0]) | (receiver == order[0]) | (tallies[receiver] == 0), 0, jnp.maximum(room, 0))
    moved = jax.random.randint(jax.random.fold_in(own, 4), (count // 2,), 0, 1 << 20) % (room + 1)
    tallies = tallies.at[source_of].add(-moved).at[receiver].add(moved)
    items = jnp.searchsorted(jnp.cumsum(tallies), jnp.arange(rows * top), side="right").astype(jnp.int32)
    table = items.reshape(top, rows).T
    table = table[jax.random.permutation(jax.random.fold_in(own, 1), rows)]
    rotation = jax.random.randint(jax.random.fold_in(own, 2), (rows, 1), 0, top)
    return jnp.take_along_axis(table, (jnp.arange(top)[None, :] + rotation) % top, axis=1)


def portions_of(number_of, total, reach, slope, full):
    portions = [(1 << 20) // math.isqrt(grade ** slope) + 1 for grade in range(1, number_of + 1)]
    largest = reach if full else min(reach, max(-(-total // number_of), total * portions[0] // sum(portions)))
    least = 1 if total - largest >= number_of - 1 else 0
    given, spare = [largest] + [least] * (number_of - 1), total - largest - least * (number_of - 1)
    while spare > 0:
        free = [i for i in range(1, number_of) if given[i] < largest] or [i for i in range(1, number_of) if given[i] < reach]
        whole, left = sum([portions[i] for i in free]), spare
        for i in free:
            more = min(reach - given[i], max(1, left * portions[i] // whole), spare)
            given[i] = given[i] + more
            spare = spare - more
    return np.array(given)


def noise(key, extent, width, reach, pieces=(), dtype=jnp.bfloat16):
    values = width * jax.random.normal(key, extent, jnp.float32)
    if pieces:
        values = values * shard_levels(key, extent, pieces, -0.22, 0.18)
    return jnp.clip(values, -reach, reach).astype(dtype)


def setup_inputs(seed: int = 0) -> dict:
    key_list = jax.random.split(jax.random.key(seed), 6)
    raw_panels = noise(key_list[0], (GROUPS, NBAS, OCC * NAUX), ((NAUX * OCC * GROUPS) ** -0.25), 0.4375, ((0, 4), (1, 8)))
    metric = noise(key_list[1], (NAUX, NAUX), NAUX ** -0.5, 0.1875)
    tile_pairs = draw_tile_pairs(jax.random.fold_in(key_list[5], 71), 0)
    owners_keys = jax.random.split(jax.random.fold_in(key_list[3], 1), NTILE // TILE_DEV)
    owners_turns = jax.random.permutation(jax.random.fold_in(key_list[3], 3), NTILE // TILE_DEV)
    owners = jax.vmap(lambda own, number: assign_block(jax.random.fold_in(key_list[3], 2), own, number, TILE_DEV, N_BLK, 1, CAP, 2))(owners_keys, owners_turns).reshape((NTILE, 1))
    group_mask = plant((jax.random.randint(key_list[4], (NTILE, GROUPS), 0, 5) < 3).astype(jnp.int32), jax.random.fold_in(key_list[4], 1), 0, 1)
    return {"raw_panels": raw_panels, "metric": metric, "tile_pairs": tile_pairs, "owners": owners, "group_mask": group_mask}


def reference(raw_panels, metric, tile_pairs, owners, group_mask):
    def transform(raw):
        flat = raw.reshape(NBAS * OCC, NAUX)
        fitted = lax.dot_general(flat, metric, (((1,), (1,)), ((), ())), preferred_element_type=jnp.float32)
        return fitted.astype(jnp.bfloat16).reshape(NBAS, OCC * NAUX)

    panels = lax.map(transform, raw_panels)
    weights = group_mask.astype(jnp.float32)

    def one_tile(item):
        pair, weight = item
        rows_mu = lax.dynamic_slice_in_dim(panels, (pair[0] * TILE).astype(jnp.int32), TILE, 1)
        rows_nu = lax.dynamic_slice_in_dim(panels, (pair[1] * TILE).astype(jnp.int32), TILE, 1)
        prods = jnp.einsum("gmk,gnk->gmn", rows_mu.astype(jnp.float32), rows_nu.astype(jnp.float32))
        return jnp.einsum("g,gmn->mn", weight, prods)

    tiles = lax.map(one_tile, (tile_pairs, weights))
    owner_ids = owners[:, 0].reshape(N_BLK, TILE_DEV)
    labels = jnp.arange(N_BLK).astype(jnp.int32)
    hits = (owner_ids[:, :, None] == labels[None, None, :]).astype(jnp.int32)
    before = jnp.cumsum(hits, axis=1) - hits
    slots = jnp.sum(before * hits, axis=2).reshape(-1).astype(jnp.int32)
    sources = (jnp.arange(N_BLK * TILE_DEV) // TILE_DEV).astype(jnp.int32)
    result = jnp.zeros((N_BLK, N_BLK, CAP, TILE, TILE), jnp.float32)
    return result.at[owners[:, 0], sources, slots].set(tiles)
```

```python
import jax
import jax.numpy as jnp
from jax import lax
from jax.experimental import pallas as pl
from jax.experimental.pallas import tpu as pltpu
from jax.sharding import PartitionSpec as P

TILE = 128
CORES = 2


def swapped(value, axis, distance):
    count = lax.axis_size(axis)
    return lax.ppermute(value, axis, [(source, source ^ distance) for source in range(count)])


def combine_kernel(block_ref, mask_ref, *refs):
    chunks, out_ref = refs[:-1], refs[-1]
    owners, slots = out_ref.shape[0], out_ref.shape[1]
    for owner in range(owners):
        for slot in range(slots):
            at = owner * slots + slot
            start = pl.multiple_of(block_ref[at] * TILE, TILE)
            total = jnp.zeros(out_ref.shape[2:], jnp.float32)
            for group, chunk in enumerate(chunks):
                weight = mask_ref[group, at].astype(jnp.float32)
                total = total + weight * chunk[:, pl.ds(start, TILE)].astype(jnp.float32)
            out_ref[owner, slot] = total


def combine(blocks, masks, chunks, owners, slots):
    rows = chunks[0].shape[0]
    smem = pl.BlockSpec(memory_space=pltpu.SMEM)
    vmem = pl.BlockSpec(memory_space=pltpu.VMEM)
    return pl.pallas_call(
        combine_kernel,
        out_shape=jax.ShapeDtypeStruct((owners, slots, rows, TILE), jnp.float32),
        in_specs=[smem, smem] + [vmem] * len(chunks),
        out_specs=vmem,
        compiler_params=pltpu.CompilerParams(vmem_limit_bytes=16 * 1024 * 1024),
    )(blocks, masks, *chunks)


def contract(left, right):
    return lax.dot_general(
        left, right, (((1,), (1,)), ((), ())), preferred_element_type=jnp.float32
    )


def per_device(raw_panels, metric, tile_pairs, owners, group_mask):
    raw = raw_panels[0]
    rows, columns = raw.shape
    naux = metric.shape[0]
    cycle = lax.axis_size("blk")
    groups = lax.axis_size("grp")
    chips = cycle // CORES
    width = columns // chips
    mine = lax.axis_index("blk")
    my_group = lax.axis_index("grp")
    my_chip = mine // CORES
    tile_count = tile_pairs.shape[0]
    capacity = max(2, 2 * tile_count // cycle)

    def piece(distance):
        return lax.dynamic_slice(raw, (jnp.int32(0), (my_chip ^ distance) * width), (rows, width))

    def fit(panel):
        parts = [
            contract(panel[:, at : at + naux], metric).astype(jnp.bfloat16)
            for at in range(0, width, naux)
        ]
        return jnp.concatenate(parts, axis=1)

    arrived = [piece(0)] + [
        swapped(piece(chip), "blk", CORES * chip) for chip in range(1, chips)
    ]

    owner_ids = owners[:, 0] ^ mine
    hits = (owner_ids[:, None] == jnp.arange(cycle)[None, :]).astype(jnp.int32)
    before = jnp.cumsum(hits, axis=0) - hits
    slots = jnp.sum(before * hits, axis=1)
    places = owner_ids * capacity + slots
    taken = (places[None, :] == jnp.arange(cycle * capacity)[:, None]).astype(jnp.int32)
    blocks = jnp.sum(taken * (tile_pairs[:, 1] ^ mine)[None, :], axis=1)
    own_mask = group_mask[:, 0]
    all_masks = [own_mask] + [swapped(own_mask, "grp", d) for d in range(1, groups)]
    masks = jnp.stack([jnp.sum(taken * mask[None, :], axis=1) for mask in all_masks])

    fitted = [fit(panel) for panel in arrived]
    beside = [swapped(panel, "blk", 1) for panel in fitted]
    everything = jnp.concatenate(
        [panel for pair in zip(fitted, beside, strict=True) for panel in pair], axis=0
    )
    slabs = [contract(panel, everything) for panel in fitted]

    total = slabs[0].reshape(rows, cycle, TILE)
    for chip in range(1, chips):
        came = swapped(slabs[chip].astype(jnp.bfloat16), "blk", CORES * chip)
        order = [block ^ (CORES * chip) for block in range(cycle)]
        came = came.reshape(rows, cycle, TILE)
        total = total + jnp.stack([came[:, block] for block in order], axis=1).astype(jnp.float32)
    total = total.reshape(rows, cycle * TILE)

    share = rows // groups

    def strip(distance):
        return lax.dynamic_slice(
            total, ((my_group ^ distance) * share, jnp.int32(0)), (share, cycle * TILE)
        )

    chunks = [strip(0)] + [
        swapped(strip(d).astype(jnp.bfloat16), "grp", d) for d in range(1, groups)
    ]
    outgoing = combine(blocks, masks, chunks, cycle, capacity)
    outgoing = outgoing.reshape(chips, CORES, capacity, share, TILE)
    crossed = swapped(outgoing[:, 1], "blk", 1)
    pairs = jnp.stack([outgoing[:, 0], crossed], axis=1)
    received = [pairs[0]] + [
        swapped(pairs[chip], "blk", CORES * chip) for chip in range(1, chips)
    ]
    by_distance = jnp.concatenate(received, axis=0)
    owned = jnp.take(by_distance, jnp.arange(cycle) ^ mine, axis=0)
    return owned[None]


def solution(mesh):
    placed = (P("grp", "blk", None), P(), P("blk", None), P("blk", None), P("blk", "grp"))
    return jax.shard_map(
        per_device,
        mesh=mesh,
        in_specs=placed,
        out_specs=P("blk", None, None, "grp", None),
        check_vma=False,
    )
```

```python
import functools

import jax
import jax.numpy as jnp
from jax import lax
from jax.experimental import pallas as pl
from jax.experimental.pallas import tpu as pltpu
from jax.sharding import PartitionSpec as P

TILE = 128
CORES = 2
MIB = 1024 * 1024
SMEM = pl.BlockSpec(memory_space=pltpu.SMEM)
VMEM = pl.BlockSpec(memory_space=pltpu.VMEM)


def swapped(value, axis, distance):
    count = lax.axis_size(axis)
    return lax.ppermute(value, axis, [(source, source ^ distance) for source in range(count)])


def shaped(shape, dtype):
    return jax.ShapeDtypeStruct(shape, dtype)


def kept(shape, dtype):
    return pltpu.VMEM(shape, dtype)


def kernel_call(body, ins, outs, out_specs, grant, scratch=()):
    return pl.pallas_call(
        body,
        out_shape=outs,
        in_specs=ins,
        out_specs=out_specs,
        scratch_shapes=scratch,
        compiler_params=pltpu.CompilerParams(vmem_limit_bytes=grant * MIB),
    )


def contract(left, right):
    return lax.dot_general(
        left, right, (((1,), (1,)), ((), ())), preferred_element_type=jnp.float32
    )


def columns(refs, start, size):
    width = refs[0].shape[1]
    return refs[start // width][:, start % width : start % width + size]


def gram(left, right):
    size = min(left[0].shape[1], right[0].shape[1])
    whole = len(left) * left[0].shape[1]
    return sum(
        contract(columns(left, at, size), columns(right, at, size))
        for at in range(0, whole, size)
    )


def unpack(refs, counts):
    groups, at = [], 0
    for count in counts:
        groups.append(refs[at : at + count])
        at += count
    return groups


def fit_kernel(count, *refs):
    panels, metric_ref, outs = refs[:count], refs[count], refs[count + 1 :]
    naux = metric_ref.shape[0]
    rows, width = panels[0].shape
    size = outs[0].shape[1]
    starts = range(0, width, naux)
    stacked = jnp.concatenate([ref[:, at : at + naux] for ref in panels for at in starts], axis=0)
    fitted = contract(stacked, metric_ref[...]).astype(jnp.bfloat16)
    for index in range(count):
        for number, out_ref in enumerate(outs):
            at = number * size
            for start in range(at, at + size, min(size, naux)):
                top = (index * len(starts) + start // naux) * rows
                from_column = start % naux
                span = min(size, naux)
                out_ref[index * rows : (index + 1) * rows, start - at : start - at + span] = fitted[
                    top : top + rows, from_column : from_column + span
                ]


def fit(panels, metric, pieces):
    rows, width = panels[0].shape
    rows_out = rows * len(panels)
    return kernel_call(
        functools.partial(fit_kernel, len(panels)),
        [VMEM] * (len(panels) + 1),
        [kept((rows_out, width // pieces), jnp.bfloat16)] * pieces,
        [VMEM] * pieces,
        8,
    )(*panels, metric)


def place(block, chip):
    spot = ((block ^ (CORES * chip)) - 1) * TILE
    return slice(spot, spot + TILE)


def put(slabs, chip, block, tile):
    if block != CORES * chip:
        slabs[chip][:, place(block, chip)] = tile.astype(slabs[chip].dtype)


def part(value, row, column):
    return value[row * TILE : (row + 1) * TILE, column * TILE : (column + 1) * TILE]


def early_kernel(counts, *refs):
    own, own_beside, others, others_beside, slabs = unpack(refs, counts)
    count = others[0].shape[0] // TILE
    put(slabs, 0, 1, gram(own, own_beside))
    outer = gram(others, own_beside)
    across = gram(own, others)
    beside = gram(own, others_beside)
    inner = gram(others, others)
    sideways = gram(others, others_beside)
    for at in range(count):
        chip = at + 1
        put(slabs, 0, CORES * chip, part(across, 0, at))
        put(slabs, 0, CORES * chip + 1, part(beside, 0, at))
        put(slabs, chip, 0, part(across, 0, at).T)
        put(slabs, chip, 1, part(outer, at, 0))
        for other in range(count):
            put(slabs, chip, CORES * (other + 1), part(inner, at, other))
            put(slabs, chip, CORES * (other + 1) + 1, part(sideways, at, other))


def early(own, own_beside, others, others_beside):
    rows = own[0].shape[0]
    chips = others[0].shape[0] // rows + 2
    span = (CORES * chips - 1) * TILE
    given = [own, own_beside, others, others_beside]
    counts = [len(pieces) for pieces in given] + [chips - 1]
    return kernel_call(
        functools.partial(early_kernel, counts),
        [VMEM] * sum(counts[:-1]),
        [kept((rows, span), jnp.bfloat16 if chip else jnp.float32) for chip in range(chips - 1)],
        [VMEM] * (chips - 1),
        12,
    )(*[piece for pieces in given for piece in pieces])


def middle_kernel(counts, *refs):
    last, own, own_beside, others, others_beside, (out_ref,) = unpack(refs, counts)
    half = others[0].shape[0]
    out_ref[:, :TILE] = gram(last, own)
    out_ref[:, TILE : 2 * TILE] = gram(last, own_beside)
    out_ref[:, 2 * TILE : 2 * TILE + half] = gram(last, others)
    out_ref[:, 2 * TILE + half :] = gram(last, others_beside)


def middle(last, own, own_beside, others, others_beside):
    rows = last[0].shape[0]
    span = 2 * (rows + others[0].shape[0])
    given = [last, own, own_beside, others, others_beside]
    counts = [len(pieces) for pieces in given] + [1]
    return kernel_call(
        functools.partial(middle_kernel, counts),
        [VMEM] * sum(counts[:-1]),
        kept((rows, span), jnp.float32),
        VMEM,
        8,
    )(*[piece for pieces in given for piece in pieces])


def late_kernel(counts, *refs):
    last, last_beside, own, others, (middle_ref,), begun, slabs = unpack(refs, counts)
    count = others[0].shape[0] // TILE
    final = count + 1
    for chip in range(final):
        slabs[chip][:, : begun[chip].shape[1]] = begun[chip][...]
    tall = gram(others, last_beside)
    put(slabs, 0, CORES * final + 1, gram(own, last_beside))
    put(slabs, final, CORES * final + 1, gram(last, last_beside))
    for core in range(CORES):
        put(slabs, final, core, middle_ref[:, core * TILE : (core + 1) * TILE])
        for at in range(count):
            spot = (CORES + core * count + at) * TILE
            put(slabs, final, CORES * (at + 1) + core, middle_ref[:, spot : spot + TILE])
    put(slabs, 0, CORES * final, middle_ref[:, :TILE].T)
    for at in range(count):
        spot = (CORES + at) * TILE
        put(slabs, at + 1, CORES * final, middle_ref[:, spot : spot + TILE].T)
        put(slabs, at + 1, CORES * final + 1, part(tall, at, 0))


def late(last, last_beside, own, others, across, begun):
    rows = own[0].shape[0]
    chips = len(begun) + 1
    span = (CORES * chips - 1) * TILE
    given = [last, last_beside, own, others, [across], begun]
    counts = [len(pieces) for pieces in given] + [chips]
    return kernel_call(
        functools.partial(late_kernel, counts),
        [VMEM] * sum(counts[:-1]),
        [kept((rows, span), jnp.bfloat16 if chip else jnp.float32) for chip in range(chips)],
        [VMEM] * chips,
        12,
    )(*[piece for pieces in given for piece in pieces])


def strips_kernel(starts_ref, weights_ref, own_ref, *refs):
    groups = starts_ref.shape[0]
    came, strips = refs[:-groups], refs[-groups:]
    share = strips[0].shape[0]
    span = own_ref.shape[1]
    for distance, strip in enumerate(strips):
        rows = pl.ds(pl.multiple_of(starts_ref[distance], share), share)
        total = own_ref[rows, :]
        for ref in came:
            total = total + ref[rows, :].astype(jnp.float32)
        strip[:, :span] = total.astype(strip.dtype)
        strip[:, span:] = weights_ref[...].astype(strip.dtype)


def strips(own, came, starts, weights):
    groups = starts.shape[0]
    rows, span = own.shape
    share = rows // groups
    whole = span + weights.shape[1]
    return kernel_call(
        strips_kernel,
        [SMEM] + [VMEM] * (2 + len(came)),
        [shaped((share, whole), jnp.bfloat16 if at else jnp.float32) for at in range(groups)],
        [VMEM] * groups,
        8,
    )(starts, weights, own, *came)


def combine_kernel(span, block_ref, *refs):
    chunks, outs = refs[:-CORES], refs[-CORES:]
    chips, slots, share = outs[0].shape[:3]
    weights = [chunk[:, span:].astype(jnp.float32) for chunk in chunks]
    for chip in range(chips):
        for core, out_ref in enumerate(outs):
            for slot in range(slots):
                at = (chip * CORES + core) * slots + slot
                start = pl.multiple_of(block_ref[at] * TILE, TILE)
                row, lanes = at % share, at // share * TILE
                total = jnp.zeros((share, TILE), jnp.float32)
                for chunk, weight in zip(chunks, weights, strict=True):
                    scale = weight[row : row + 1, lanes : lanes + TILE]
                    total = total + scale * chunk[:, pl.ds(start, TILE)].astype(jnp.float32)
                out_ref[chip, slot] = total


def combine(blocks, chunks, span, chips, slots):
    share = chunks[0].shape[0]
    return kernel_call(
        functools.partial(combine_kernel, span),
        [SMEM] + [VMEM] * len(chunks),
        [shaped((chips, slots, share, TILE), jnp.float32)] * CORES,
        [VMEM] * CORES,
        8,
    )(blocks, *chunks)


def settle_kernel(mine_ref, *refs):
    pieces, out_ref = refs[:-1], refs[-1]
    mine = mine_ref[0]
    for chip, piece in enumerate(pieces):
        for core in range(CORES):
            out_ref[mine ^ (chip * CORES + core)] = piece[core]


def settle(mine, pieces):
    shape = (CORES * len(pieces), *pieces[0].shape[1:])
    return kernel_call(
        settle_kernel,
        [SMEM] + [VMEM] * len(pieces),
        shaped(shape, jnp.float32),
        VMEM,
        8,
    )(mine, *pieces)


def per_device(raw_panels, metric, tile_pairs, owners, group_mask):
    raw = raw_panels[0]
    rows, columns = raw.shape
    cycle = lax.axis_size("blk")
    groups = lax.axis_size("grp")
    chips = cycle // CORES
    width = columns // chips
    mine = lax.axis_index("blk")
    my_group = lax.axis_index("grp")
    tile_count = tile_pairs.shape[0]
    capacity = max(2, 2 * tile_count // cycle)
    final = chips - 1
    share = rows // groups

    def piece(source, chip):
        start = ((mine // CORES) ^ chip) * width
        return lax.dynamic_slice(source, (jnp.int32(0), start), (rows, width))

    def beside(pieces):
        return [swapped(piece, "blk", 1) for piece in pieces]

    pieces = [piece(raw, chip) for chip in range(1, final)]
    arrived = [swapped(value, "blk", CORES * (at + 1)) for at, value in enumerate(pieces)]
    raw = lax.optimization_barrier((raw, *pieces))[0]
    own = fit([piece(raw, 0)], metric, 2)
    own_beside = beside(own)
    last_piece = lax.optimization_barrier((piece(raw, final), *own_beside))[0]
    last = swapped(last_piece, "blk", CORES * final)

    others = fit(arrived, metric, 4)
    others_beside = beside(others)
    begun = early(own, own_beside, others, others_beside)

    own_mask, pairs, owner_ids = lax.optimization_barrier(
        (group_mask[:, 0], tile_pairs, owners[:, 0], *own)
    )[:3]
    owner_ids = owner_ids ^ mine
    hits = (owner_ids[:, None] == jnp.arange(cycle)[None, :]).astype(jnp.int32)
    before = jnp.cumsum(hits, axis=0) - hits
    slots = jnp.sum(before * hits, axis=1)
    places = owner_ids * capacity + slots
    taken = (places[None, :] == jnp.arange(cycle * capacity)[:, None]).astype(jnp.int32)
    blocks = jnp.maximum(jnp.sum(taken * (pairs[:, 1] ^ mine)[None, :], axis=1) - 1, 0)
    weights = jnp.sum(taken * own_mask[None, :], axis=1).astype(jnp.float32)
    tall = -(-weights.shape[0] // share) * share
    weights = jnp.pad(weights, (0, tall - weights.shape[0])).reshape(-1, share).T
    weights = jnp.repeat(weights, TILE, axis=1)

    last, blocks, weights = lax.optimization_barrier((last, blocks, weights, *begun))[:3]
    last_fitted = fit([last], metric, 2)
    last_beside = beside(last_fitted)
    across = middle(last_fitted, own, own_beside, others, others_beside)
    slabs = late(last_fitted, last_beside, own, others, across, begun)

    came = [swapped(slabs[chip], "blk", CORES * chip) for chip in range(1, chips)]
    strip_starts = (my_group ^ jnp.arange(groups, dtype=jnp.int32)) * share
    own_strips = strips(slabs[0], came, strip_starts, weights)
    chunks = [own_strips[0]] + [swapped(own_strips[d], "grp", d) for d in range(1, groups)]

    straight, crossing = combine(blocks, chunks, slabs[0].shape[1], chips, capacity)
    crossed = swapped(crossing, "blk", 1)
    paired = jnp.stack([straight, crossed], axis=1)
    received = [paired[0]] + [
        swapped(paired[chip], "blk", CORES * chip) for chip in range(1, chips)
    ]
    return settle(mine[None], received)[None]


def solution(mesh):
    placed = (P("grp", "blk", None), P(), P("blk", None), P("blk", None), P("blk", "grp"))
    return jax.shard_map(
        per_device,
        mesh=mesh,
        in_specs=placed,
        out_specs=P("blk", None, None, "grp", None),
        check_vma=False,
    )
```

```python
import functools

import jax
import jax.numpy as jnp
from jax import lax
from jax.experimental import pallas as pl
from jax.experimental.pallas import tpu as pltpu
from jax.sharding import PartitionSpec as P

TILE = 128
CORES = 2
MIB = 1024 * 1024
SMEM = pl.BlockSpec(memory_space=pltpu.SMEM)
VMEM = pl.BlockSpec(memory_space=pltpu.VMEM)
HBM = pl.BlockSpec(memory_space=pltpu.HBM)
ANY = pl.BlockSpec(memory_space=pl.ANY)


def swapped(value, axis, distance):
    count = lax.axis_size(axis)
    return lax.ppermute(value, axis, [(source, source ^ distance) for source in range(count)])


def shaped(shape, dtype):
    return jax.ShapeDtypeStruct(shape, dtype)


def kept(shape, dtype):
    return pltpu.VMEM(shape, dtype)


def kernel_call(body, ins, outs, out_specs, grant, scratch=()):
    return pl.pallas_call(
        body,
        out_shape=outs,
        in_specs=ins,
        out_specs=out_specs,
        scratch_shapes=scratch,
        compiler_params=pltpu.CompilerParams(vmem_limit_bytes=grant * MIB),
    )


def contract(left, right):
    return lax.dot_general(
        left, right, (((1,), (1,)), ((), ())), preferred_element_type=jnp.float32
    )


def columns(refs, start, size):
    width = refs[0].shape[1]
    return refs[start // width][:, start % width : start % width + size]


def gram(left, right):
    size = min(left[0].shape[1], right[0].shape[1])
    whole = len(left) * left[0].shape[1]
    return sum(
        contract(columns(left, at, size), columns(right, at, size))
        for at in range(0, whole, size)
    )


def unpack(refs, counts):
    groups, at = [], 0
    for count in counts:
        groups.append(refs[at : at + count])
        at += count
    return groups


def write_fitted(panels, metric, outs):
    naux = metric.shape[0]
    rows, width = panels[0].shape
    size = outs[0].shape[1]
    span = min(size, naux)
    starts = range(0, width, naux)
    stacked = jnp.concatenate([ref[:, at : at + naux] for ref in panels for at in starts], axis=0)
    fitted = contract(stacked, metric).astype(jnp.bfloat16)
    for index in range(len(panels)):
        for at in range(0, width, span):
            top = (index * len(starts) + at // naux) * rows
            left = at % naux
            outs[at // size][index * rows : (index + 1) * rows, at % size : at % size + span] = (
                fitted[top : top + rows, left : left + span]
            )


def fit_kernel(count, pieces, *refs):
    outs = refs[-pieces:]
    write_fitted(refs[:count][::-1], refs[count][...], outs)
    below = outs[0].shape[0] - count * refs[0].shape[0]
    if below:
        for ref, out_ref in zip(refs[count + 1 : count + 1 + pieces], outs, strict=True):
            out_ref[out_ref.shape[0] - below :] = ref[...]


def fit(panels, metric, pieces, below=(), before=()):
    rows, width = panels[0].shape
    rows_out = rows * len(panels) + (below[0].shape[0] if below else 0)
    return kernel_call(
        functools.partial(fit_kernel, len(panels), pieces),
        [VMEM] * (len(panels) + 1 + len(below)) + [ANY] * len(before),
        [kept((rows_out, width // pieces), jnp.bfloat16)] * pieces,
        [VMEM] * pieces,
        8,
    )(*panels[::-1], metric, *below, *before)


def copy_all(pairs, arrived):
    copies = [
        pltpu.make_async_copy(source, target, arrived.at[at])
        for at, (source, target) in enumerate(pairs)
    ]
    for copy in copies:
        copy.start()
    for copy in copies:
        copy.wait()


def column_block(raw_ref, start_ref, at, width):
    return raw_ref.at[:, pl.ds(pl.multiple_of(start_ref[at], width), width)]


def cut_kernel(count, starts_ref, raw_ref, *refs):
    pieces, token_ref, arrived = refs[-count - 2 : -2], refs[-2], refs[-1]
    width = pieces[0].shape[1]
    copy_all(
        [(column_block(raw_ref, starts_ref, at, width), piece) for at, piece in enumerate(pieces)],
        arrived,
    )
    token_ref[0] = jnp.int32(0)


def cut(raw, starts, width, *before):
    rows = raw.shape[0]
    count = len(starts)
    *pieces, token = kernel_call(
        functools.partial(cut_kernel, count),
        [SMEM, HBM] + [ANY] * len(before),
        [kept((rows, width), raw.dtype)] * count + [shaped((1,), jnp.int32)],
        [VMEM] * count + [SMEM],
        4,
        [pltpu.SemaphoreType.DMA((count,))],
    )(jnp.stack(starts), raw, *before)
    return pieces, token


def first_fit_kernel(token_ref, starts_ref, raw_ref, metric_ref, *refs):
    held_ref, outs, (own_ref, arrived) = refs[0], refs[1:-2], refs[-2:]
    width = own_ref.shape[1]
    copy_all(
        [(column_block(raw_ref, starts_ref, 0, width), own_ref), (metric_ref, held_ref)], arrived
    )
    write_fitted([own_ref], held_ref[...], outs)


def first_fit(token, raw, metric, start, width, pieces):
    rows = raw.shape[0]
    held, *fitted = kernel_call(
        first_fit_kernel,
        [SMEM, SMEM, HBM, HBM],
        [kept(metric.shape, metric.dtype)]
        + [kept((rows, width // pieces), jnp.bfloat16)] * pieces,
        [VMEM] * (pieces + 1),
        8,
        [pltpu.VMEM((rows, width), raw.dtype), pltpu.SemaphoreType.DMA((2,))],
    )(token, start[None], raw, pltpu.with_memory_space_constraint(metric, pltpu.HBM))
    return held, fitted


def place(block, chip):
    spot = ((block ^ (CORES * chip)) - 1) * TILE
    return slice(spot, spot + TILE)


def put(slabs, chip, block, tile):
    if block != CORES * chip:
        slabs[chip][:, place(block, chip)] = tile.astype(slabs[chip].dtype)


def part(value, row, column):
    return value[row * TILE : (row + 1) * TILE, column * TILE : (column + 1) * TILE]


def early_kernel(counts, *refs):
    own, own_beside, others, others_beside, slabs = unpack(refs, counts)
    count = others[0].shape[0] // TILE
    put(slabs, 0, 1, gram(own, own_beside))
    outer = gram(others, own_beside)
    across = gram(own, others)
    beside = gram(own, others_beside)
    inner = gram(others, others)
    sideways = gram(others, others_beside)
    for at in range(count):
        chip = at + 1
        put(slabs, 0, CORES * chip, part(across, 0, at))
        put(slabs, 0, CORES * chip + 1, part(beside, 0, at))
        put(slabs, chip, 0, part(across, 0, at).T)
        put(slabs, chip, 1, part(outer, at, 0))
        for other in range(count):
            put(slabs, chip, CORES * (other + 1), part(inner, at, other))
            put(slabs, chip, CORES * (other + 1) + 1, part(sideways, at, other))


def early(own, own_beside, others, others_beside):
    rows = own[0].shape[0]
    chips = others[0].shape[0] // rows + 2
    span = (CORES * chips - 1) * TILE
    given = [own, own_beside, others, others_beside]
    counts = [len(pieces) for pieces in given] + [chips - 1]
    return kernel_call(
        functools.partial(early_kernel, counts),
        [VMEM] * sum(counts[:-1]),
        [kept((rows, span), jnp.bfloat16 if chip else jnp.float32) for chip in range(chips - 1)],
        [VMEM] * (chips - 1),
        12,
    )(*[piece for pieces in given for piece in pieces])


def middle_kernel(counts, *refs):
    last, own, own_beside, others, others_beside, (out_ref,) = unpack(refs, counts)
    half = others[0].shape[0]
    out_ref[:, :TILE] = gram(last, own)
    out_ref[:, TILE : 2 * TILE] = gram(last, own_beside)
    out_ref[:, 2 * TILE : 2 * TILE + half] = gram(last, others)
    out_ref[:, 2 * TILE + half :] = gram(last, others_beside)


def middle(last, own, own_beside, others, others_beside):
    rows = last[0].shape[0]
    span = 2 * (rows + others[0].shape[0])
    given = [last, own, own_beside, others, others_beside]
    counts = [len(pieces) for pieces in given] + [1]
    return kernel_call(
        functools.partial(middle_kernel, counts),
        [VMEM] * sum(counts[:-1]),
        kept((rows, span), jnp.float32),
        VMEM,
        8,
    )(*[piece for pieces in given for piece in pieces])


def late_kernel(counts, *refs):
    last, last_beside, own, others, (middle_ref,), begun, slabs = unpack(refs, counts)
    count = others[0].shape[0] // TILE
    final = count + 1
    for chip in range(final):
        slabs[chip][:, : begun[chip].shape[1]] = begun[chip][...]
    tall = gram(others, last_beside)
    put(slabs, 0, CORES * final + 1, gram(own, last_beside))
    put(slabs, final, CORES * final + 1, gram(last, last_beside))
    for core in range(CORES):
        put(slabs, final, core, middle_ref[:, core * TILE : (core + 1) * TILE])
        for at in range(count):
            spot = (CORES + core * count + at) * TILE
            put(slabs, final, CORES * (at + 1) + core, middle_ref[:, spot : spot + TILE])
    put(slabs, 0, CORES * final, middle_ref[:, :TILE].T)
    for at in range(count):
        spot = (CORES + at) * TILE
        put(slabs, at + 1, CORES * final, middle_ref[:, spot : spot + TILE].T)
        put(slabs, at + 1, CORES * final + 1, part(tall, at, 0))


def late(last, last_beside, own, others, across, begun):
    rows = own[0].shape[0]
    chips = len(begun) + 1
    span = (CORES * chips - 1) * TILE
    given = [last, last_beside, own, others, [across], begun]
    counts = [len(pieces) for pieces in given] + [chips]
    return kernel_call(
        functools.partial(late_kernel, counts),
        [VMEM] * sum(counts[:-1]),
        [kept((rows, span), jnp.bfloat16 if chip else jnp.float32) for chip in range(chips)],
        [VMEM] * chips,
        12,
    )(*[piece for pieces in given for piece in pieces])


def strips_kernel(starts_ref, weights_ref, own_ref, *refs):
    groups = starts_ref.shape[0]
    came, strips = refs[:-groups], refs[-groups:]
    share = strips[0].shape[0]
    span = own_ref.shape[1]
    for distance, strip in enumerate(strips):
        rows = pl.ds(pl.multiple_of(starts_ref[distance], share), share)
        total = own_ref[rows, :]
        for ref in came:
            total = total + ref[rows, :].astype(jnp.float32)
        strip[:, :span] = total.astype(strip.dtype)
        strip[:, span:] = weights_ref[...].astype(strip.dtype)


def strips(own, came, starts, weights):
    groups = starts.shape[0]
    rows, span = own.shape
    share = rows // groups
    whole = span + weights.shape[1]
    return kernel_call(
        strips_kernel,
        [SMEM] + [VMEM] * (2 + len(came)),
        [shaped((share, whole), jnp.bfloat16 if at else jnp.float32) for at in range(groups)],
        [VMEM] * groups,
        8,
    )(starts, weights, own, *came)


def combine_kernel(span, block_ref, *refs):
    chunks, (home_ref, straight_ref, crossing_ref) = refs[:-3], refs[-3:]
    slots, share = home_ref.shape[:2]
    weights = [chunk[:, span:].astype(jnp.float32) for chunk in chunks]
    for owner in range(crossing_ref.shape[0] * CORES):
        chip, core = owner // CORES, owner % CORES
        for slot in range(slots):
            at = owner * slots + slot
            start = pl.multiple_of(block_ref[at] * TILE, TILE)
            row, lanes = at % share, at // share * TILE
            total = jnp.zeros((share, TILE), jnp.float32)
            for chunk, weight in zip(chunks, weights, strict=True):
                scale = weight[row : row + 1, lanes : lanes + TILE]
                total = total + scale * chunk[:, pl.ds(start, TILE)].astype(jnp.float32)
            if owner == 0:
                home_ref[slot] = total
            elif core == 0:
                straight_ref[chip - 1, slot] = total.astype(jnp.bfloat16)
            else:
                crossing_ref[chip, slot] = total.astype(jnp.bfloat16)


def combine(blocks, chunks, span, chips, slots):
    share = chunks[0].shape[0]
    return kernel_call(
        functools.partial(combine_kernel, span),
        [SMEM] + [VMEM] * len(chunks),
        [
            shaped((slots, share, TILE), jnp.float32),
            shaped((chips - 1, slots, share, TILE), jnp.bfloat16),
            shaped((chips, slots, share, TILE), jnp.bfloat16),
        ],
        [VMEM] * 3,
        8,
    )(blocks, *chunks)


def settle_kernel(mine_ref, home_ref, beside_ref, *refs):
    came, out_ref = refs[:-1], refs[-1]
    mine = mine_ref[0]
    out_ref[mine] = home_ref[...]
    out_ref[mine ^ 1] = beside_ref[...].astype(jnp.float32)
    for at, piece in enumerate(came):
        for core in range(CORES):
            out_ref[mine ^ ((at + 1) * CORES + core)] = piece[core].astype(jnp.float32)


def settle(mine, home, from_beside, came):
    return kernel_call(
        settle_kernel,
        [SMEM] + [VMEM] * (2 + len(came)),
        shaped((CORES * (len(came) + 1), *home.shape), jnp.float32),
        VMEM,
        8,
    )(mine, home, from_beside, *came)


def per_device(raw_panels, metric, tile_pairs, owners, group_mask):
    raw = pltpu.with_memory_space_constraint(raw_panels[0], pltpu.HBM)
    rows, columns = raw.shape
    cycle = lax.axis_size("blk")
    groups = lax.axis_size("grp")
    chips = cycle // CORES
    width = columns // chips
    mine = lax.axis_index("blk")
    my_group = lax.axis_index("grp")
    tile_count = tile_pairs.shape[0]
    capacity = max(2, 2 * tile_count // cycle)
    final = chips - 1
    share = rows // groups

    def beside(pieces):
        return [swapped(piece, "blk", 1) for piece in pieces]

    starts = [((mine // CORES) ^ chip) * width for chip in range(chips)]
    pieces, token = cut(raw, starts[1:final], width)
    arrived = [swapped(piece, "blk", CORES * (at + 1)) for at, piece in enumerate(pieces)]
    metric, own = first_fit(token, raw, metric, starts[0], width, 2)
    own_beside = beside(own)
    (last_piece,), token = cut(raw, starts[final:], width, *own_beside)
    last = swapped(last_piece, "blk", CORES * final)

    own_mask, pairs, owner_ids = lax.optimization_barrier(
        (group_mask[:, 0], tile_pairs, owners[:, 0], token)
    )[:3]
    owner_ids = owner_ids ^ mine
    hits = (owner_ids[:, None] == jnp.arange(cycle)[None, :]).astype(jnp.int32)
    before = jnp.cumsum(hits, axis=0) - hits
    slots = jnp.sum(before * hits, axis=1)
    places = owner_ids * capacity + slots
    taken = (places[None, :] == jnp.arange(cycle * capacity)[:, None]).astype(jnp.int32)
    blocks = jnp.maximum(jnp.sum(taken * (pairs[:, 1] ^ mine)[None, :], axis=1) - 1, 0)
    weights = jnp.sum(taken * own_mask[None, :], axis=1).astype(jnp.float32)
    tall = -(-weights.shape[0] // share) * share
    weights = jnp.pad(weights, (0, tall - weights.shape[0])).reshape(-1, share).T
    weights = jnp.repeat(weights, TILE, axis=1)

    others = fit(arrived, metric, 4)
    others_beside = beside(others)
    begun = early(own, own_beside, others, others_beside)

    last_fitted = fit([last], metric, 2, (), (blocks, weights, begun[0]))
    last_beside = beside(last_fitted)
    across = middle(last_fitted, own, own_beside, others, others_beside)
    slabs = late(last_fitted, last_beside, own, others, across, begun)

    came = [swapped(slabs[chip], "blk", CORES * chip) for chip in range(1, chips)]
    strip_starts = (my_group ^ jnp.arange(groups, dtype=jnp.int32)) * share
    own_strips = strips(slabs[0], came, strip_starts, weights)
    chunks = [own_strips[0]] + [swapped(own_strips[d], "grp", d) for d in range(1, groups)]

    home, straight, crossing = combine(blocks, chunks, slabs[0].shape[1], chips, capacity)
    crossed = swapped(crossing, "blk", 1)
    paired = jnp.stack([straight, crossed[1:]], axis=1)
    received = [
        swapped(paired[chip - 1], "blk", CORES * chip) for chip in range(1, chips)
    ]
    return settle(mine[None], home, crossed[0], received)[None]


def solution(mesh):
    placed = (P("grp", "blk", None), P(), P("blk", None), P("blk", None), P("blk", "grp"))
    return jax.shard_map(
        per_device,
        mesh=mesh,
        in_specs=placed,
        out_specs=P("blk", None, None, "grp", None),
        check_vma=False,
    )
```

```python
import functools

import jax
import jax.numpy as jnp
from jax import lax
from jax.experimental import pallas as pl
from jax.experimental.pallas import tpu as pltpu
from jax.sharding import PartitionSpec as P

TILE = 128
CORES = 2
MIB = 1024 * 1024
MIDDLE_WEIGHT = 60 * 10**8
HOME_WEIGHT = 12 * 10**8
SMEM = pl.BlockSpec(memory_space=pltpu.SMEM)
VMEM = pl.BlockSpec(memory_space=pltpu.VMEM)
HBM = pl.BlockSpec(memory_space=pltpu.HBM)
ANY = pl.BlockSpec(memory_space=pl.ANY)


def swapped(value, axis, distance):
    count = lax.axis_size(axis)
    return lax.ppermute(value, axis, [(source, source ^ distance) for source in range(count)])


def shaped(shape, dtype):
    return jax.ShapeDtypeStruct(shape, dtype)


def kept(shape, dtype):
    return pltpu.VMEM(shape, dtype)


def kernel_call(body, ins, outs, out_specs, grant, scratch=(), weight=None):
    return pl.pallas_call(
        body,
        out_shape=outs,
        in_specs=ins,
        out_specs=out_specs,
        scratch_shapes=scratch,
        compiler_params=pltpu.CompilerParams(vmem_limit_bytes=grant * MIB),
        cost_estimate=weight
        and pl.CostEstimate(flops=weight, bytes_accessed=MIB, transcendentals=0),
    )


def contract(left, right):
    return lax.dot_general(
        left, right, (((1,), (1,)), ((), ())), preferred_element_type=jnp.float32
    )


def columns(refs, start, size):
    width = refs[0].shape[1]
    return refs[start // width][:, start % width : start % width + size]


def gram(left, right):
    size = min(left[0].shape[1], right[0].shape[1])
    whole = len(left) * left[0].shape[1]
    return sum(
        contract(columns(left, at, size), columns(right, at, size))
        for at in range(0, whole, size)
    )


def unpack(refs, counts):
    groups, at = [], 0
    for count in counts:
        groups.append(refs[at : at + count])
        at += count
    return groups


def write_fitted(panels, metric, outs):
    naux = metric.shape[0]
    rows, width = panels[0].shape
    size = outs[0].shape[1]
    span = min(size, naux)
    starts = range(0, width, naux)
    stacked = jnp.concatenate([ref[:, at : at + naux] for ref in panels for at in starts], axis=0)
    fitted = contract(stacked, metric).astype(jnp.bfloat16)
    for index in range(len(panels)):
        for at in range(0, width, span):
            top = (index * len(starts) + at // naux) * rows
            left = at % naux
            outs[at // size][index * rows : (index + 1) * rows, at % size : at % size + span] = (
                fitted[top : top + rows, left : left + span]
            )


def fit_kernel(count, pieces, *refs):
    outs = refs[-pieces:]
    write_fitted(refs[:count][::-1], refs[count][...], outs)
    below = outs[0].shape[0] - count * refs[0].shape[0]
    if below:
        for ref, out_ref in zip(refs[count + 1 : count + 1 + pieces], outs, strict=True):
            out_ref[out_ref.shape[0] - below :] = ref[...]


def fit(panels, metric, pieces, below=(), before=()):
    rows, width = panels[0].shape
    rows_out = rows * len(panels) + (below[0].shape[0] if below else 0)
    return kernel_call(
        functools.partial(fit_kernel, len(panels), pieces),
        [VMEM] * (len(panels) + 1 + len(below)) + [ANY] * len(before),
        [kept((rows_out, width // pieces), jnp.bfloat16)] * pieces,
        [VMEM] * pieces,
        8,
    )(*panels[::-1], metric, *below, *before)


def copy_all(pairs, arrived):
    copies = [
        pltpu.make_async_copy(source, target, arrived.at[at])
        for at, (source, target) in enumerate(pairs)
    ]
    for copy in copies:
        copy.start()
    for copy in copies:
        copy.wait()


def column_block(raw_ref, start_ref, at, width):
    return raw_ref.at[:, pl.ds(pl.multiple_of(start_ref[at], width), width)]


def cut_kernel(count, starts_ref, raw_ref, *refs):
    pieces, token_ref, arrived = refs[-count - 2 : -2], refs[-2], refs[-1]
    width = pieces[0].shape[1]
    copy_all(
        [(column_block(raw_ref, starts_ref, at, width), piece) for at, piece in enumerate(pieces)],
        arrived,
    )
    token_ref[0] = jnp.int32(0)


def cut(raw, starts, width, *before):
    rows = raw.shape[0]
    count = len(starts)
    *pieces, token = kernel_call(
        functools.partial(cut_kernel, count),
        [SMEM, HBM] + [ANY] * len(before),
        [kept((rows, width), raw.dtype)] * count + [shaped((1,), jnp.int32)],
        [VMEM] * count + [SMEM],
        4,
        [pltpu.SemaphoreType.DMA((count,))],
    )(jnp.stack(starts), raw, *before)
    return pieces, token


def first_fit_kernel(token_ref, starts_ref, raw_ref, metric_ref, *refs):
    held_ref, outs, (own_ref, arrived) = refs[0], refs[1:-2], refs[-2:]
    width = own_ref.shape[1]
    copy_all(
        [(column_block(raw_ref, starts_ref, 0, width), own_ref), (metric_ref, held_ref)], arrived
    )
    write_fitted([own_ref], held_ref[...], outs)


def first_fit(token, raw, metric, start, width, pieces):
    rows = raw.shape[0]
    held, *fitted = kernel_call(
        first_fit_kernel,
        [SMEM, SMEM, HBM, HBM],
        [kept(metric.shape, metric.dtype)]
        + [kept((rows, width // pieces), jnp.bfloat16)] * pieces,
        [VMEM] * (pieces + 1),
        8,
        [pltpu.VMEM((rows, width), raw.dtype), pltpu.SemaphoreType.DMA((2,))],
    )(token, start[None], raw, pltpu.with_memory_space_constraint(metric, pltpu.HBM))
    return held, fitted


def spot(number):
    return slice(number * TILE, (number + 1) * TILE)


def place(block, chip):
    return (block ^ (CORES * chip)) - 1


def early_blocks(chip, final):
    return [block for block in range(CORES * final) if block != CORES * chip]


def part(value, row, column):
    return value[spot(row), spot(column)]


def early_kernel(counts, *refs):
    own, own_beside, others, others_beside, slabs = unpack(refs, counts)
    final = len(slabs)
    count = others[0].shape[0] // TILE
    across = gram(own, others)
    beside = gram(own, others_beside)
    outer = gram(others, own_beside)
    inner = gram(others, others)
    sideways = gram(others, others_beside)
    tiles = {(0, 1): gram(own, own_beside)}
    for at in range(count):
        chip = at + 1
        tiles[0, CORES * chip] = part(across, 0, at)
        tiles[0, CORES * chip + 1] = part(beside, 0, at)
        tiles[chip, 0] = part(across, 0, at).T
        tiles[chip, 1] = part(outer, at, 0)
        for other in range(count):
            tiles[chip, CORES * (other + 1)] = part(inner, at, other)
            tiles[chip, CORES * (other + 1) + 1] = part(sideways, at, other)
    for chip, slab in enumerate(slabs):
        for at, block in enumerate(early_blocks(chip, final)):
            where = place(block, chip) if chip == 0 else at
            slab[:, spot(where)] = tiles[chip, block].astype(slab.dtype)


def early(own, own_beside, others, others_beside):
    final = others[0].shape[0] // TILE + 1
    span = (CORES * final - 1) * TILE
    given = [own, own_beside, others, others_beside]
    counts = [len(pieces) for pieces in given] + [final]
    return kernel_call(
        functools.partial(early_kernel, counts),
        [VMEM] * sum(counts[:-1]),
        [kept((TILE, span), jnp.bfloat16 if chip else jnp.float32) for chip in range(final)],
        [VMEM] * final,
        12,
    )(*[piece for pieces in given for piece in pieces])


def middle_kernel(counts, *refs):
    last, own, own_beside, others, others_beside, (out_ref,) = unpack(refs, counts)
    half = others[0].shape[0]
    out_ref[:, :TILE] = gram(last, own)
    out_ref[:, TILE : 2 * TILE] = gram(last, own_beside)
    out_ref[:, 2 * TILE : 2 * TILE + half] = gram(last, others)
    out_ref[:, 2 * TILE + half :] = gram(last, others_beside)


def middle(last, own, own_beside, others, others_beside):
    rows = last[0].shape[0]
    span = 2 * (rows + others[0].shape[0])
    given = [last, own, own_beside, others, others_beside]
    counts = [len(pieces) for pieces in given] + [1]
    return kernel_call(
        functools.partial(middle_kernel, counts),
        [VMEM] * sum(counts[:-1]),
        kept((rows, span), jnp.float32),
        VMEM,
        8,
        weight=MIDDLE_WEIGHT,
    )(*[piece for pieces in given for piece in pieces])


def late_kernel(counts, *refs):
    last, last_beside, own, others, (middle_ref,), slabs, (side_ref,) = unpack(refs, counts)
    final = len(slabs)
    last_slab = slabs[-1]
    tall = gram(others, last_beside)
    side_ref[...] = gram(own, last_beside)
    tile = gram(last, last_beside)
    last_slab[:, spot(place(CORES * final + 1, final))] = tile.astype(jnp.bfloat16)
    for chip in range(final):
        straight = middle_ref[:, spot(chip + 1 if chip else 0)]
        sideways = middle_ref[:, spot(chip + final if chip else 1)]
        last_slab[:, spot(place(CORES * chip, final))] = straight.astype(jnp.bfloat16)
        last_slab[:, spot(place(CORES * chip + 1, final))] = sideways.astype(jnp.bfloat16)
        if chip:
            slabs[chip - 1][:, spot(0)] = straight.T.astype(jnp.bfloat16)
            slabs[chip - 1][:, spot(1)] = part(tall, chip - 1, 0).astype(jnp.bfloat16)


def late(last, last_beside, own, others, across):
    final = others[0].shape[0] // TILE + 1
    span = (CORES * final + 1) * TILE
    given = [last, last_beside, own, others, [across]]
    counts = [len(pieces) for pieces in given] + [final, 1]
    return kernel_call(
        functools.partial(late_kernel, counts),
        [VMEM] * sum(counts[:-2]),
        [kept((TILE, CORES * TILE), jnp.bfloat16)] * (final - 1)
        + [kept((TILE, span), jnp.bfloat16), kept((TILE, TILE), jnp.float32)],
        [VMEM] * (final + 1),
        12,
    )(*[piece for pieces in given for piece in pieces])


def home_kernel(counts, *refs):
    (middle_ref, side_ref, begun), came, (own_slab,) = unpack(refs, counts)
    final = len(came) + 1

    def with_early(tile, block):
        for at, ref in enumerate(came):
            seen = block ^ (CORES * (at + 1))
            blocks = early_blocks(at + 1, final)
            if seen in blocks:
                tile = tile + ref[:, spot(blocks.index(seen))].astype(jnp.float32)
        own_slab[:, spot(place(block, 0))] = tile

    for block in early_blocks(0, final):
        with_early(begun[:, spot(place(block, 0))], block)
    with_early(middle_ref[:, spot(0)].T, CORES * final)
    with_early(side_ref[...], CORES * final + 1)


def home_slab(across, side, begun, came):
    span = (CORES * (len(came) + 2) - 1) * TILE
    given = [[across, side, begun], came]
    counts = [len(pieces) for pieces in given] + [1]
    return kernel_call(
        functools.partial(home_kernel, counts),
        [VMEM] * sum(counts[:-1]),
        kept((TILE, span), jnp.float32),
        VMEM,
        8,
        weight=HOME_WEIGHT,
    )(*[piece for pieces in given for piece in pieces])


def strips_kernel(starts_ref, weights_ref, own_ref, *refs):
    groups = starts_ref.shape[0]
    (last_came, *came), strips = refs[:-groups], refs[-groups:]
    final = len(came) + 1
    share = strips[0].shape[0]
    span = own_ref.shape[1]
    for distance, strip in enumerate(strips):
        rows = pl.ds(pl.multiple_of(starts_ref[distance], share), share)
        strip[:, span:] = weights_ref[...].astype(strip.dtype)
        for number in range(span // TILE):
            total = own_ref[rows, spot(number)]
            total = total + last_came[rows, spot(number)].astype(jnp.float32)
            for at, ref in enumerate(came):
                core = ((number + 1) ^ (CORES * (at + 1))) - CORES * final
                if core in range(CORES):
                    total = total + ref[rows, spot(core)].astype(jnp.float32)
            strip[:, spot(number)] = total.astype(strip.dtype)


def strips(own, came, starts, weights):
    groups = starts.shape[0]
    rows, span = own.shape
    share = rows // groups
    whole = span + weights.shape[1]
    return kernel_call(
        strips_kernel,
        [SMEM] + [VMEM] * (2 + len(came)),
        [shaped((share, whole), jnp.bfloat16 if at else jnp.float32) for at in range(groups)],
        [VMEM] * groups,
        8,
    )(starts, weights, own, *came)


def combine_kernel(span, block_ref, *refs):
    chunks, (home_ref, straight_ref, crossing_ref) = refs[:-3], refs[-3:]
    slots, share = home_ref.shape[:2]
    weights = [chunk[:, span:].astype(jnp.float32) for chunk in chunks]
    for owner in range(crossing_ref.shape[0] * CORES):
        chip, core = owner // CORES, owner % CORES
        for slot in range(slots):
            at = owner * slots + slot
            start = pl.multiple_of(block_ref[at] * TILE, TILE)
            row, lanes = at % share, at // share * TILE
            total = jnp.zeros((share, TILE), jnp.float32)
            for chunk, weight in zip(chunks, weights, strict=True):
                scale = weight[row : row + 1, lanes : lanes + TILE]
                total = total + scale * chunk[:, pl.ds(start, TILE)].astype(jnp.float32)
            if owner == 0:
                home_ref[slot] = total
            elif core == 0:
                straight_ref[chip - 1, slot] = total.astype(jnp.bfloat16)
            else:
                crossing_ref[chip, slot] = total.astype(jnp.bfloat16)


def combine(blocks, chunks, span, chips, slots):
    share = chunks[0].shape[0]
    return kernel_call(
        functools.partial(combine_kernel, span),
        [SMEM] + [VMEM] * len(chunks),
        [
            shaped((slots, share, TILE), jnp.float32),
            shaped((chips - 1, slots, share, TILE), jnp.bfloat16),
            shaped((chips, slots, share, TILE), jnp.bfloat16),
        ],
        [VMEM] * 3,
        8,
    )(blocks, *chunks)


def settle_kernel(mine_ref, home_ref, beside_ref, *refs):
    came, out_ref = refs[:-1], refs[-1]
    mine = mine_ref[0]
    out_ref[mine] = home_ref[...]
    out_ref[mine ^ 1] = beside_ref[...].astype(jnp.float32)
    for at, piece in enumerate(came):
        for core in range(CORES):
            out_ref[mine ^ ((at + 1) * CORES + core)] = piece[core].astype(jnp.float32)


def settle(mine, home, from_beside, came):
    return kernel_call(
        settle_kernel,
        [SMEM] + [VMEM] * (2 + len(came)),
        shaped((CORES * (len(came) + 1), *home.shape), jnp.float32),
        VMEM,
        8,
    )(mine, home, from_beside, *came)


def per_device(raw_panels, metric, tile_pairs, owners, group_mask):
    raw = pltpu.with_memory_space_constraint(raw_panels[0], pltpu.HBM)
    rows, columns = raw.shape
    cycle = lax.axis_size("blk")
    groups = lax.axis_size("grp")
    chips = cycle // CORES
    width = columns // chips
    mine = lax.axis_index("blk")
    my_group = lax.axis_index("grp")
    tile_count = tile_pairs.shape[0]
    capacity = max(2, 2 * tile_count // cycle)
    final = chips - 1
    share = rows // groups

    def beside(pieces):
        return [swapped(piece, "blk", 1) for piece in pieces]

    starts = [((mine // CORES) ^ chip) * width for chip in range(chips)]
    pieces, token = cut(raw, starts[1:final], width)
    arrived = [swapped(piece, "blk", CORES * (at + 1)) for at, piece in enumerate(pieces)]
    metric, own = first_fit(token, raw, metric, starts[0], width, 2)
    own_beside = beside(own)
    (last_piece,), token = cut(raw, starts[final:], width, *own_beside)
    last = swapped(last_piece, "blk", CORES * final)

    own_mask, pairs, owner_ids = lax.optimization_barrier(
        (group_mask[:, 0], tile_pairs, owners[:, 0], token)
    )[:3]
    owner_ids = owner_ids ^ mine
    hits = (owner_ids[:, None] == jnp.arange(cycle)[None, :]).astype(jnp.int32)
    before = jnp.cumsum(hits, axis=0) - hits
    slots = jnp.sum(before * hits, axis=1)
    places = owner_ids * capacity + slots
    taken = (places[None, :] == jnp.arange(cycle * capacity)[:, None]).astype(jnp.int32)
    blocks = jnp.maximum(jnp.sum(taken * (pairs[:, 1] ^ mine)[None, :], axis=1) - 1, 0)
    weights = jnp.sum(taken * own_mask[None, :], axis=1).astype(jnp.float32)
    tall = -(-weights.shape[0] // share) * share
    weights = jnp.pad(weights, (0, tall - weights.shape[0])).reshape(-1, share).T
    weights = jnp.repeat(weights, TILE, axis=1)

    others = fit(arrived, metric, 4)
    others_beside = beside(others)
    begun = early(own, own_beside, others, others_beside)
    came_early = [swapped(begun[chip], "blk", CORES * chip) for chip in range(1, final)]

    last_fitted = fit([last], metric, 2, (), (blocks, weights, begun[0]))
    last_beside = beside(last_fitted)
    across = middle(last_fitted, own, own_beside, others, others_beside)
    *slabs, side = late(last_fitted, last_beside, own, others, across)
    came = [
        swapped(slabs[chip - 1], "blk", CORES * chip) for chip in (final, *range(1, final))
    ]
    own_slab = home_slab(across, side, begun[0], came_early)
    strip_starts = (my_group ^ jnp.arange(groups, dtype=jnp.int32)) * share
    own_strips = strips(own_slab, came, strip_starts, weights)
    chunks = [own_strips[0]] + [swapped(own_strips[d], "grp", d) for d in range(1, groups)]

    home, straight, crossing = combine(blocks, [chunks[-1], *chunks[1:-1], chunks[0]], own_slab.shape[1], chips, capacity)
    crossed = swapped(crossing, "blk", 1)
    paired = jnp.stack([straight, crossed[1:]], axis=1)
    received = [
        swapped(paired[chip - 1], "blk", CORES * chip) for chip in range(1, chips)
    ]
    return settle(mine[None], home, crossed[0], received)[None]


def solution(mesh):
    placed = (P("grp", "blk", None), P(), P("blk", None), P("blk", None), P("blk", "grp"))
    return jax.shard_map(
        per_device,
        mesh=mesh,
        in_specs=placed,
        out_specs=P("blk", None, None, "grp", None),
        check_vma=False,
    )
```

```python
import functools

import jax
import jax.numpy as jnp
from jax import lax
from jax.experimental import pallas as pl
from jax.experimental.pallas import tpu as pltpu
from jax.sharding import PartitionSpec as P

TILE = 128
CORES = 2
MIB = 1024 * 1024
MIDDLE_WEIGHT = 60 * 10**8
LATE_WEIGHT = 5 * 10**9
HOME_WEIGHT = 12 * 10**8
SMEM = pl.BlockSpec(memory_space=pltpu.SMEM)
VMEM = pl.BlockSpec(memory_space=pltpu.VMEM)
HBM = pl.BlockSpec(memory_space=pltpu.HBM)
ANY = pl.BlockSpec(memory_space=pl.ANY)


def swapped(value, axis, distance):
    count = lax.axis_size(axis)
    return lax.ppermute(value, axis, [(source, source ^ distance) for source in range(count)])


def shaped(shape, dtype):
    return jax.ShapeDtypeStruct(shape, dtype)


def kept(shape, dtype):
    return pltpu.VMEM(shape, dtype)


def kernel_call(body, ins, outs, out_specs, grant, scratch=(), weight=None):
    return pl.pallas_call(
        body,
        out_shape=outs,
        in_specs=ins,
        out_specs=out_specs,
        scratch_shapes=scratch,
        compiler_params=pltpu.CompilerParams(vmem_limit_bytes=grant * MIB),
        cost_estimate=weight
        and pl.CostEstimate(flops=weight, bytes_accessed=MIB, transcendentals=0),
    )


def contract(left, right):
    return lax.dot_general(
        left, right, (((1,), (1,)), ((), ())), preferred_element_type=jnp.float32
    )


def columns(refs, start, size):
    width = refs[0].shape[1]
    return refs[start // width][:, start % width : start % width + size]


def gram(left, right):
    size = min(left[0].shape[1], right[0].shape[1])
    whole = len(left) * left[0].shape[1]
    return sum(
        contract(columns(left, at, size), columns(right, at, size))
        for at in range(0, whole, size)
    )


def unpack(refs, counts):
    groups, at = [], 0
    for count in counts:
        groups.append(refs[at : at + count])
        at += count
    return groups


def write_fitted(panels, metric, outs):
    naux = metric.shape[0]
    rows, width = panels[0].shape
    size = outs[0].shape[1]
    span = min(size, naux)
    starts = range(0, width, naux)
    stacked = jnp.concatenate([ref[:, at : at + naux] for ref in panels for at in starts], axis=0)
    fitted = contract(stacked, metric).astype(jnp.bfloat16)
    for index in range(len(panels)):
        for at in range(0, width, span):
            top = (index * len(starts) + at // naux) * rows
            left = at % naux
            outs[at // size][index * rows : (index + 1) * rows, at % size : at % size + span] = (
                fitted[top : top + rows, left : left + span]
            )


def fit_kernel(count, pieces, *refs):
    outs = refs[-pieces:]
    write_fitted(refs[:count], refs[count][...], outs)
    below = outs[0].shape[0] - count * refs[0].shape[0]
    if below:
        for ref, out_ref in zip(refs[count + 1 : count + 1 + pieces], outs, strict=True):
            out_ref[out_ref.shape[0] - below :] = ref[...]


def fit(panels, metric, pieces, below=(), before=()):
    rows, width = panels[0].shape
    rows_out = rows * len(panels) + (below[0].shape[0] if below else 0)
    return kernel_call(
        functools.partial(fit_kernel, len(panels), pieces),
        [VMEM] * (len(panels) + 1 + len(below)) + [ANY] * len(before),
        [kept((rows_out, width // pieces), jnp.bfloat16)] * pieces,
        [VMEM] * pieces,
        8,
    )(*panels, metric, *below, *before)


def copy_all(pairs, arrived):
    copies = [
        pltpu.make_async_copy(source, target, arrived.at[at])
        for at, (source, target) in enumerate(pairs)
    ]
    for copy in copies:
        copy.start()
    for copy in copies:
        copy.wait()


def column_block(raw_ref, start_ref, at, width):
    return raw_ref.at[:, pl.ds(pl.multiple_of(start_ref[at], width), width)]


def cut_kernel(count, starts_ref, raw_ref, *refs):
    pieces, token_ref, arrived = refs[-count - 2 : -2], refs[-2], refs[-1]
    width = pieces[0].shape[1]
    copy_all(
        [(column_block(raw_ref, starts_ref, at, width), piece) for at, piece in enumerate(pieces)],
        arrived,
    )
    token_ref[0] = jnp.int32(0)


def cut(raw, starts, width, *before):
    rows = raw.shape[0]
    count = len(starts)
    *pieces, token = kernel_call(
        functools.partial(cut_kernel, count),
        [SMEM, HBM] + [ANY] * len(before),
        [kept((rows, width), raw.dtype)] * count + [shaped((1,), jnp.int32)],
        [VMEM] * count + [SMEM],
        4,
        [pltpu.SemaphoreType.DMA((count,))],
    )(jnp.stack(starts), raw, *before)
    return pieces, token


def first_fit_kernel(starts_ref, raw_ref, metric_ref, *refs):
    held_ref, outs, (own_ref, arrived) = refs[0], refs[1:-2], refs[-2:]
    width = own_ref.shape[1]
    copy_all(
        [(column_block(raw_ref, starts_ref, 0, width), own_ref), (metric_ref, held_ref)], arrived
    )
    write_fitted([own_ref], held_ref[...], outs)


def first_fit(raw, metric, start, width, pieces):
    rows = raw.shape[0]
    held, *fitted = kernel_call(
        first_fit_kernel,
        [SMEM, HBM, HBM],
        [kept(metric.shape, metric.dtype)]
        + [kept((rows, width // pieces), jnp.bfloat16)] * pieces,
        [VMEM] * (pieces + 1),
        8,
        [pltpu.VMEM((rows, width), raw.dtype), pltpu.SemaphoreType.DMA((2,))],
    )(start[None], raw, pltpu.with_memory_space_constraint(metric, pltpu.HBM))
    return held, fitted


def spot(number):
    return slice(number * TILE, (number + 1) * TILE)


def place(block, chip):
    return (block ^ (CORES * chip)) - 1


def early_blocks(chip, final):
    return [block for block in range(CORES * final) if block != CORES * chip]


def part(value, row, column):
    return value[spot(row), spot(column)]


def early_kernel(counts, *refs):
    own, own_beside, others, others_beside, slabs = unpack(refs, counts)
    final = len(slabs)
    count = others[0].shape[0] // TILE
    across = gram(own, others)
    beside = gram(own, others_beside)
    outer = gram(others, own_beside)
    inner = gram(others, others)
    sideways = gram(others, others_beside)
    tiles = {(0, 1): gram(own, own_beside)}
    for at in range(count):
        chip = at + 1
        tiles[0, CORES * chip] = part(across, 0, at)
        tiles[0, CORES * chip + 1] = part(beside, 0, at)
        tiles[chip, 0] = part(across, 0, at).T
        tiles[chip, 1] = part(outer, at, 0)
        for other in range(count):
            tiles[chip, CORES * (other + 1)] = part(inner, at, other)
            tiles[chip, CORES * (other + 1) + 1] = part(sideways, at, other)
    for chip, slab in enumerate(slabs):
        for at, block in enumerate(early_blocks(chip, final)):
            where = place(block, chip) if chip == 0 else at
            slab[:, spot(where)] = tiles[chip, block].astype(slab.dtype)


def early(own, own_beside, others, others_beside):
    final = others[0].shape[0] // TILE + 1
    span = (CORES * final - 1) * TILE
    given = [own, own_beside, others, others_beside]
    counts = [len(pieces) for pieces in given] + [final]
    return kernel_call(
        functools.partial(early_kernel, counts),
        [VMEM] * sum(counts[:-1]),
        [kept((TILE, span), jnp.bfloat16 if chip else jnp.float32) for chip in range(final)],
        [VMEM] * final,
        12,
    )(*[piece for pieces in given for piece in pieces])


def middle_kernel(counts, *refs):
    last, own, own_beside, others, others_beside, (out_ref,) = unpack(refs, counts)
    half = others[0].shape[0]
    out_ref[:, :TILE] = gram(last, own)
    out_ref[:, TILE : 2 * TILE] = gram(last, own_beside)
    out_ref[:, 2 * TILE : 2 * TILE + half] = gram(last, others)
    out_ref[:, 2 * TILE + half :] = gram(last, others_beside)


def middle(last, own, own_beside, others, others_beside):
    rows = last[0].shape[0]
    span = 2 * (rows + others[0].shape[0])
    given = [last, own, own_beside, others, others_beside]
    counts = [len(pieces) for pieces in given] + [1]
    return kernel_call(
        functools.partial(middle_kernel, counts),
        [VMEM] * sum(counts[:-1]),
        kept((rows, span), jnp.float32),
        VMEM,
        8,
        weight=MIDDLE_WEIGHT,
    )(*[piece for pieces in given for piece in pieces])


def last_slab_kernel(counts, *refs):
    last, last_beside, (middle_ref,), (slab,) = unpack(refs, counts)
    final = middle_ref.shape[1] // (CORES * TILE)
    tile = gram(last, last_beside)
    slab[:, spot(place(CORES * final + 1, final))] = tile.astype(jnp.bfloat16)
    for chip in range(final):
        straight = middle_ref[:, spot(chip + 1 if chip else 0)]
        sideways = middle_ref[:, spot(chip + final if chip else 1)]
        slab[:, spot(place(CORES * chip, final))] = straight.astype(jnp.bfloat16)
        slab[:, spot(place(CORES * chip + 1, final))] = sideways.astype(jnp.bfloat16)


def last_chip_slab(last, last_beside, across):
    given = [last, last_beside, [across]]
    counts = [len(pieces) for pieces in given] + [1]
    return kernel_call(
        functools.partial(last_slab_kernel, counts),
        [VMEM] * sum(counts[:-1]),
        kept((TILE, across.shape[1] + TILE), jnp.bfloat16),
        VMEM,
        8,
    )(*[piece for pieces in given for piece in pieces])


def late_kernel(counts, *refs):
    last_beside, own, others, (middle_ref,), slabs, (side_ref,) = unpack(refs, counts)
    tall = gram(others, last_beside)
    side_ref[...] = gram(own, last_beside)
    for at, slab in enumerate(slabs):
        slab[:, spot(0)] = middle_ref[:, spot(at + 2)].T.astype(jnp.bfloat16)
        slab[:, spot(1)] = part(tall, at, 0).astype(jnp.bfloat16)


def late(last_beside, own, others, across):
    chips = others[0].shape[0] // TILE
    given = [last_beside, own, others, [across]]
    counts = [len(pieces) for pieces in given] + [chips, 1]
    return kernel_call(
        functools.partial(late_kernel, counts),
        [VMEM] * sum(counts[:-2]),
        [kept((TILE, CORES * TILE), jnp.bfloat16)] * chips + [kept((TILE, TILE), jnp.float32)],
        [VMEM] * (chips + 1),
        8,
        weight=LATE_WEIGHT,
    )(*[piece for pieces in given for piece in pieces])


def home_kernel(counts, *refs):
    (middle_ref, side_ref, begun), came, (own_slab,) = unpack(refs, counts)
    final = len(came) + 1

    def with_early(tile, block):
        for at, ref in enumerate(came):
            seen = block ^ (CORES * (at + 1))
            blocks = early_blocks(at + 1, final)
            if seen in blocks:
                tile = tile + ref[:, spot(blocks.index(seen))].astype(jnp.float32)
        own_slab[:, spot(place(block, 0))] = tile

    for block in early_blocks(0, final):
        with_early(begun[:, spot(place(block, 0))], block)
    with_early(middle_ref[:, spot(0)].T, CORES * final)
    with_early(side_ref[...], CORES * final + 1)


def home_slab(across, side, begun, came):
    span = (CORES * (len(came) + 2) - 1) * TILE
    given = [[across, side, begun], came]
    counts = [len(pieces) for pieces in given] + [1]
    return kernel_call(
        functools.partial(home_kernel, counts),
        [VMEM] * sum(counts[:-1]),
        kept((TILE, span), jnp.float32),
        VMEM,
        8,
        weight=HOME_WEIGHT,
    )(*[piece for pieces in given for piece in pieces])


def strips_kernel(groups, weights_ref, own_ref, *refs):
    my_group = lax.axis_index("grp")
    (last_came, *came), strips = refs[:-groups], refs[-groups:]
    final = len(came) + 1
    share = strips[0].shape[0]
    span = own_ref.shape[1]
    for distance, strip in enumerate(strips):
        rows = pl.ds(pl.multiple_of((my_group ^ distance) * share, share), share)
        strip[:, span:] = weights_ref[...].astype(strip.dtype)
        for number in range(span // TILE):
            total = own_ref[rows, spot(number)]
            total = total + last_came[rows, spot(number)].astype(jnp.float32)
            for at, ref in enumerate(came):
                core = ((number + 1) ^ (CORES * (at + 1))) - CORES * final
                if core in range(CORES):
                    total = total + ref[rows, spot(core)].astype(jnp.float32)
            strip[:, spot(number)] = total.astype(strip.dtype)


def strips(own, came, groups, weights):
    rows, span = own.shape
    share = rows // groups
    whole = span + weights.shape[1]
    return kernel_call(
        functools.partial(strips_kernel, groups),
        [VMEM] * (2 + len(came)),
        [shaped((share, whole), jnp.bfloat16 if at else jnp.float32) for at in range(groups)],
        [VMEM] * groups,
        8,
    )(weights, own, *came)


def combine_kernel(owners, span, block_ref, *refs):
    chunks, outs = refs[: -len(owners)], refs[-len(owners) :]
    slots, share = outs[0].shape[1:3]
    weights = [chunk[:, span:].astype(jnp.float32) for chunk in chunks]
    for out_ref, held in zip(outs, owners, strict=True):
        for number, owner in enumerate(held):
            for slot in range(slots):
                at = owner * slots + slot
                start = pl.multiple_of(block_ref[at] * TILE, TILE)
                row, lanes = at % share, at // share * TILE
                total = jnp.zeros((share, TILE), jnp.float32)
                for chunk, weight in zip(chunks, weights, strict=True):
                    scale = weight[row : row + 1, lanes : lanes + TILE]
                    total = total + scale * chunk[:, pl.ds(start, TILE)].astype(jnp.float32)
                out_ref[number, slot] = total.astype(out_ref.dtype)


def combine(owners, blocks, chunks, span, slots):
    share = chunks[0].shape[0]
    return kernel_call(
        functools.partial(combine_kernel, owners, span),
        [SMEM] + [VMEM] * len(chunks),
        [
            shaped((len(held), slots, share, TILE), jnp.bfloat16 if any(held) else jnp.float32)
            for held in owners
        ],
        [VMEM] * len(owners),
        8,
    )(blocks, *chunks)


def scalars_kernel(values_ref, out_ref):
    for at in range(values_ref.shape[0]):
        out_ref[at] = values_ref[at]


def scalars(values):
    return kernel_call(
        scalars_kernel, [SMEM], pltpu.SMEM(values.shape, values.dtype), SMEM, 1
    )(values)


def settle_kernel(order, home_ref, beside_ref, *refs):
    came, out_ref = refs[:-1], refs[-1]
    mine = lax.axis_index("blk")
    out_ref[mine] = home_ref[...]
    out_ref[mine ^ 1] = beside_ref[...].astype(jnp.float32)
    for chip, piece in zip(order, came, strict=True):
        for core in range(CORES):
            out_ref[mine ^ (chip * CORES + core)] = piece[core].astype(jnp.float32)


def settle(home, from_beside, came, order):
    return kernel_call(
        functools.partial(settle_kernel, order),
        [VMEM] * (2 + len(came)),
        shaped((CORES * (len(came) + 1), *home.shape), jnp.float32),
        VMEM,
        8,
    )(home, from_beside, *came)


def per_device(raw_panels, metric, tile_pairs, owners, group_mask):
    raw = pltpu.with_memory_space_constraint(raw_panels[0], pltpu.HBM)
    rows, columns = raw.shape
    cycle = lax.axis_size("blk")
    groups = lax.axis_size("grp")
    chips = cycle // CORES
    width = columns // chips
    mine = lax.axis_index("blk")
    tile_count = tile_pairs.shape[0]
    capacity = max(2, 2 * tile_count // cycle)
    final = chips - 1
    share = rows // groups

    def beside(pieces):
        return [swapped(piece, "blk", 1) for piece in pieces]

    starts = [((mine // CORES) ^ chip) * width for chip in range(chips)]
    pieces = [
        lax.dynamic_slice(raw_panels[0], (jnp.int32(0), starts[chip]), (rows, width))
        for chip in range(1, final)
    ]
    arrived = [swapped(piece, "blk", CORES * (at + 1)) for at, piece in enumerate(pieces)]
    metric, own = first_fit(raw, metric, starts[0], width, 1)
    own_beside = beside(own)
    (last_piece,), token = cut(raw, starts[final:], width, *own_beside)
    last = swapped(last_piece, "blk", CORES * final)

    own_mask, pairs, owner_ids = lax.optimization_barrier(
        (group_mask[:, 0], tile_pairs, owners[:, 0], token)
    )[:3]
    owner_ids = owner_ids ^ mine
    hits = (owner_ids[:, None] == jnp.arange(cycle)[None, :]).astype(jnp.int32)
    before = jnp.cumsum(hits, axis=0) - hits
    slots = jnp.sum(before * hits, axis=1)
    places = owner_ids * capacity + slots
    taken = (places[None, :] == jnp.arange(cycle * capacity)[:, None]).astype(jnp.int32)
    blocks = scalars(jnp.maximum(jnp.sum(taken * (pairs[:, 1] ^ mine)[None, :], axis=1) - 1, 0))
    weights = jnp.sum(taken * own_mask[None, :], axis=1).astype(jnp.float32)
    tall = -(-weights.shape[0] // share) * share
    weights = jnp.pad(weights, (0, tall - weights.shape[0])).reshape(-1, share).T
    weights = jnp.repeat(weights, TILE, axis=1)

    others = fit(arrived, metric, 4)
    others_beside = beside(others)
    begun = early(own, own_beside, others, others_beside)
    came_early = [swapped(begun[chip], "blk", CORES * chip) for chip in range(1, final)]

    last_fitted = fit([last], metric, 2, (), (blocks, weights, begun[0]))
    last_beside = beside(last_fitted)
    across = middle(last_fitted, own, own_beside, others, others_beside)
    last_slab = last_chip_slab(last_fitted, last_beside, across)
    *slabs, side = late(last_beside, own, others, across)
    came = [swapped(last_slab, "blk", CORES * final)] + [
        swapped(slabs[chip - 1], "blk", CORES * chip) for chip in range(1, final)
    ]
    own_slab = home_slab(across, side, begun[0], came_early)
    own_strips = strips(own_slab, came, groups, weights)
    chunks = [own_strips[0]] + [swapped(own_strips[d], "grp", d) for d in range(1, groups)]

    chunks = [*chunks[2:], chunks[1], chunks[0]]
    span = own_slab.shape[1]
    (crossing,) = combine([range(1, cycle, CORES)], blocks, chunks, span, capacity)
    crossed = swapped(crossing, "blk", 1)
    own_owners = [range(1), range(CORES, cycle, CORES)]
    home, straight = combine(own_owners, blocks, chunks, span, capacity)
    paired = jnp.stack([straight, crossed[1:]], axis=1)
    order = (final, *range(1, final))
    received = [swapped(paired[chip - 1], "blk", CORES * chip) for chip in order]
    return settle(home[0], crossed[0], received, order)[None]


def solution(mesh):
    placed = (P("grp", "blk", None), P(), P("blk", None), P("blk", None), P("blk", "grp"))
    return jax.shard_map(
        per_device,
        mesh=mesh,
        in_specs=placed,
        out_specs=P("blk", None, None, "grp", None),
        check_vma=False,
    )
```

```python
import functools

import jax
import jax.numpy as jnp
from jax import lax
from jax.experimental import pallas as pl
from jax.experimental.pallas import tpu as pltpu
from jax.sharding import PartitionSpec as P

TILE = 128
CORES = 2
MIB = 1024 * 1024
MIDDLE_WEIGHT = 60 * 10**8
LATE_WEIGHT = 5 * 10**9
HOME_WEIGHT = 12 * 10**8
SMEM = pl.BlockSpec(memory_space=pltpu.SMEM)
VMEM = pl.BlockSpec(memory_space=pltpu.VMEM)
HBM = pl.BlockSpec(memory_space=pltpu.HBM)
ANY = pl.BlockSpec(memory_space=pl.ANY)


def swapped(value, axis, distance):
    count = lax.axis_size(axis)
    return lax.ppermute(value, axis, [(source, source ^ distance) for source in range(count)])


def shaped(shape, dtype):
    return jax.ShapeDtypeStruct(shape, dtype)


def kept(shape, dtype):
    return pltpu.VMEM(shape, dtype)


def kernel_call(body, ins, outs, out_specs, grant, scratch=(), weight=None):
    return pl.pallas_call(
        body,
        out_shape=outs,
        in_specs=ins,
        out_specs=out_specs,
        scratch_shapes=scratch,
        compiler_params=pltpu.CompilerParams(vmem_limit_bytes=grant * MIB),
        cost_estimate=weight
        and pl.CostEstimate(flops=weight, bytes_accessed=MIB, transcendentals=0),
    )


def contract(left, right):
    return lax.dot_general(
        left, right, (((1,), (1,)), ((), ())), preferred_element_type=jnp.float32
    )


def columns(refs, start, size):
    width = refs[0].shape[1]
    return refs[start // width][:, start % width : start % width + size]


def gram(left, right):
    size = min(left[0].shape[1], right[0].shape[1])
    whole = len(left) * left[0].shape[1]
    return sum(
        contract(columns(left, at, size), columns(right, at, size))
        for at in range(0, whole, size)
    )


def unpack(refs, counts):
    groups, at = [], 0
    for count in counts:
        groups.append(refs[at : at + count])
        at += count
    return groups


def write_fitted(panels, metric, outs):
    naux = metric.shape[0]
    rows, width = panels[0].shape
    size = outs[0].shape[1]
    span = min(size, naux)
    starts = range(0, width, naux)
    stacked = jnp.concatenate([ref[:, at : at + naux] for ref in panels for at in starts], axis=0)
    fitted = contract(stacked, metric).astype(jnp.bfloat16)
    for index in range(len(panels)):
        for at in range(0, width, span):
            top = (index * len(starts) + at // naux) * rows
            left = at % naux
            outs[at // size][index * rows : (index + 1) * rows, at % size : at % size + span] = (
                fitted[top : top + rows, left : left + span]
            )


def fit_kernel(count, pieces, *refs):
    outs = refs[-pieces:]
    write_fitted(refs[:count], refs[count][...], outs)
    below = outs[0].shape[0] - count * refs[0].shape[0]
    if below:
        for ref, out_ref in zip(refs[count + 1 : count + 1 + pieces], outs, strict=True):
            out_ref[out_ref.shape[0] - below :] = ref[...]


def fit(panels, metric, pieces, below=(), before=()):
    rows, width = panels[0].shape
    rows_out = rows * len(panels) + (below[0].shape[0] if below else 0)
    return kernel_call(
        functools.partial(fit_kernel, len(panels), pieces),
        [VMEM] * (len(panels) + 1 + len(below)) + [ANY] * len(before),
        [kept((rows_out, width // pieces), jnp.bfloat16)] * pieces,
        [VMEM] * pieces,
        8,
    )(*panels, metric, *below, *before)


def copy_all(pairs, arrived):
    copies = [
        pltpu.make_async_copy(source, target, arrived.at[at])
        for at, (source, target) in enumerate(pairs)
    ]
    for copy in copies:
        copy.start()
    for copy in copies:
        copy.wait()


def column_block(raw_ref, start_ref, at, width):
    return raw_ref.at[:, pl.ds(pl.multiple_of(start_ref[at], width), width)]


def cut_kernel(count, starts_ref, raw_ref, *refs):
    pieces, token_ref, arrived = refs[-count - 2 : -2], refs[-2], refs[-1]
    width = pieces[0].shape[1]
    copy_all(
        [(column_block(raw_ref, starts_ref, at, width), piece) for at, piece in enumerate(pieces)],
        arrived,
    )
    token_ref[0] = jnp.int32(0)


def cut(raw, starts, width, *before):
    rows = raw.shape[0]
    count = len(starts)
    *pieces, token = kernel_call(
        functools.partial(cut_kernel, count),
        [SMEM, HBM] + [ANY] * len(before),
        [kept((rows, width), raw.dtype)] * count + [shaped((1,), jnp.int32)],
        [VMEM] * count + [SMEM],
        4,
        [pltpu.SemaphoreType.DMA((count,))],
    )(jnp.stack(starts), raw, *before)
    return pieces, token


def first_fit_kernel(starts_ref, raw_ref, metric_ref, *refs):
    held_ref, outs, (own_ref, arrived) = refs[0], refs[1:-2], refs[-2:]
    width = own_ref.shape[1]
    copy_all(
        [(column_block(raw_ref, starts_ref, 0, width), own_ref), (metric_ref, held_ref)], arrived
    )
    write_fitted([own_ref], held_ref[...], outs)


def first_fit(raw, metric, start, width, pieces):
    rows = raw.shape[0]
    held, *fitted = kernel_call(
        first_fit_kernel,
        [SMEM, HBM, HBM],
        [kept(metric.shape, metric.dtype)]
        + [kept((rows, width // pieces), jnp.bfloat16)] * pieces,
        [VMEM] * (pieces + 1),
        8,
        [pltpu.VMEM((rows, width), raw.dtype), pltpu.SemaphoreType.DMA((2,))],
    )(start[None], raw, pltpu.with_memory_space_constraint(metric, pltpu.HBM))
    return held, fitted


def spot(number):
    return slice(number * TILE, (number + 1) * TILE)


def place(block, chip):
    return (block ^ (CORES * chip)) - 1


def early_blocks(chip, final):
    return [block for block in range(CORES * final) if block != CORES * chip]


def part(value, row, column):
    return value[spot(row), spot(column)]


def early_kernel(counts, *refs):
    own, own_beside, others, others_beside, slabs = unpack(refs, counts)
    final = len(slabs)
    count = others[0].shape[0] // TILE
    across = gram(own, others)
    beside = gram(own, others_beside)
    outer = gram(others, own_beside)
    inner = gram(others, others)
    sideways = gram(others, others_beside)
    tiles = {(0, 1): gram(own, own_beside)}
    for at in range(count):
        chip = at + 1
        tiles[0, CORES * chip] = part(across, 0, at)
        tiles[0, CORES * chip + 1] = part(beside, 0, at)
        tiles[chip, 0] = part(across, 0, at).T
        tiles[chip, 1] = part(outer, at, 0)
        for other in range(count):
            tiles[chip, CORES * (other + 1)] = part(inner, at, other)
            tiles[chip, CORES * (other + 1) + 1] = part(sideways, at, other)
    for chip, slab in enumerate(slabs):
        for at, block in enumerate(early_blocks(chip, final)):
            where = place(block, chip) if chip == 0 else at
            slab[:, spot(where)] = tiles[chip, block].astype(slab.dtype)


def early(own, own_beside, others, others_beside):
    final = others[0].shape[0] // TILE + 1
    span = (CORES * final - 1) * TILE
    given = [own, own_beside, others, others_beside]
    counts = [len(pieces) for pieces in given] + [final]
    return kernel_call(
        functools.partial(early_kernel, counts),
        [VMEM] * sum(counts[:-1]),
        [kept((TILE, span), jnp.bfloat16 if chip else jnp.float32) for chip in range(final)],
        [VMEM] * final,
        12,
    )(*[piece for pieces in given for piece in pieces])


def middle_kernel(counts, *refs):
    last, own, own_beside, others, others_beside, (slab, straight_ref) = unpack(refs, counts)
    final = straight_ref.shape[1] // TILE
    straight = [gram(last, own)]
    sideways = [gram(last, own_beside)]
    wide = gram(last, others)
    straight += [part(wide, 0, at) for at in range(final - 1)]
    wide = gram(last, others_beside)
    sideways += [part(wide, 0, at) for at in range(final - 1)]
    for chip in range(final):
        straight_ref[:, spot(chip)] = straight[chip]
        slab[:, spot(CORES * chip)] = straight[chip].astype(slab.dtype)
        slab[:, spot(CORES * chip + 1)] = sideways[chip].astype(slab.dtype)


def middle(last, own, own_beside, others, others_beside):
    final = others[0].shape[0] // TILE + 1
    given = [last, own, own_beside, others, others_beside]
    counts = [len(pieces) for pieces in given] + [2]
    return kernel_call(
        functools.partial(middle_kernel, counts),
        [VMEM] * sum(counts[:-1]),
        [
            kept((TILE, CORES * final * TILE), jnp.bfloat16),
            kept((TILE, final * TILE), jnp.float32),
        ],
        [VMEM] * 2,
        8,
        weight=MIDDLE_WEIGHT,
    )(*[piece for pieces in given for piece in pieces])


def late_kernel(counts, *refs):
    last, last_beside, own, others, (straight_ref,), slabs, (side_ref,) = unpack(refs, counts)
    tall = gram(others, last_beside)
    side_ref[...] = gram(own, last_beside)
    *slabs, corner = slabs
    corner[...] = gram(last, last_beside).astype(corner.dtype)
    for at, slab in enumerate(slabs):
        slab[:, spot(0)] = straight_ref[:, spot(at + 1)].T.astype(slab.dtype)
        slab[:, spot(1)] = part(tall, at, 0).astype(slab.dtype)


def late(last, last_beside, own, others, straight):
    chips = others[0].shape[0] // TILE
    given = [last, last_beside, own, others, [straight]]
    counts = [len(pieces) for pieces in given] + [chips + 1, 1]
    return kernel_call(
        functools.partial(late_kernel, counts),
        [VMEM] * sum(counts[:-2]),
        [kept((TILE, CORES * TILE), jnp.bfloat16)] * chips
        + [kept((TILE, TILE), jnp.bfloat16), kept((TILE, TILE), jnp.float32)],
        [VMEM] * (chips + 2),
        8,
        weight=LATE_WEIGHT,
    )(*[piece for pieces in given for piece in pieces])


def home_kernel(counts, *refs):
    (middle_ref, side_ref, begun), came, (own_slab,) = unpack(refs, counts)
    final = len(came) + 1

    def with_early(tile, block):
        for at, ref in enumerate(came):
            seen = block ^ (CORES * (at + 1))
            blocks = early_blocks(at + 1, final)
            if seen in blocks:
                tile = tile + ref[:, spot(blocks.index(seen))].astype(jnp.float32)
        own_slab[:, spot(place(block, 0))] = tile

    for block in early_blocks(0, final):
        with_early(begun[:, spot(place(block, 0))], block)
    with_early(middle_ref[:, spot(0)].T, CORES * final)
    with_early(side_ref[...], CORES * final + 1)


def home_slab(across, side, begun, came):
    span = (CORES * (len(came) + 2) - 1) * TILE
    given = [[across, side, begun], came]
    counts = [len(pieces) for pieces in given] + [1]
    return kernel_call(
        functools.partial(home_kernel, counts),
        [VMEM] * sum(counts[:-1]),
        kept((TILE, span), jnp.float32),
        VMEM,
        8,
        weight=HOME_WEIGHT,
    )(*[piece for pieces in given for piece in pieces])


def strips_kernel(groups, weights_ref, own_ref, *refs):
    my_group = lax.axis_index("grp")
    (last_came, corner, *came), strips = refs[:-groups], refs[-groups:]
    final = len(came) + 1
    share = strips[0].shape[0]
    span = own_ref.shape[1]
    for distance, strip in enumerate(strips):
        rows = pl.ds(pl.multiple_of((my_group ^ distance) * share, share), share)
        strip[:, span:] = weights_ref[...].astype(strip.dtype)
        for number in range(span // TILE):
            total = own_ref[rows, spot(number)]
            block = (number + 1) ^ (CORES * final)
            if block < CORES * final:
                total = total + last_came[rows, spot(block)].astype(jnp.float32)
            else:
                total = total + corner[rows, :].astype(jnp.float32)
            for at, ref in enumerate(came):
                core = ((number + 1) ^ (CORES * (at + 1))) - CORES * final
                if core in range(CORES):
                    total = total + ref[rows, spot(core)].astype(jnp.float32)
            strip[:, spot(number)] = total.astype(strip.dtype)


def strips(own, came, groups, weights):
    rows, span = own.shape
    share = rows // groups
    whole = span + weights.shape[1]
    return kernel_call(
        functools.partial(strips_kernel, groups),
        [VMEM] * (2 + len(came)),
        [shaped((share, whole), jnp.bfloat16 if at else jnp.float32) for at in range(groups)],
        [VMEM] * groups,
        8,
    )(weights, own, *came)


def combine_kernel(owners, span, block_ref, *refs):
    chunks, outs = refs[: -len(owners)], refs[-len(owners) :]
    slots, share = outs[0].shape[1:3]
    weights = [chunk[:, span:].astype(jnp.float32) for chunk in chunks]
    for out_ref, held in zip(outs, owners, strict=True):
        for number, owner in enumerate(held):
            for slot in range(slots):
                at = owner * slots + slot
                start = pl.multiple_of(block_ref[at] * TILE, TILE)
                row, lanes = at % share, at // share * TILE
                total = jnp.zeros((share, TILE), jnp.float32)
                for chunk, weight in zip(chunks, weights, strict=True):
                    scale = weight[row : row + 1, lanes : lanes + TILE]
                    total = total + scale * chunk[:, pl.ds(start, TILE)].astype(jnp.float32)
                out_ref[number, slot] = total.astype(out_ref.dtype)


def combine(owners, blocks, chunks, span, slots):
    share = chunks[0].shape[0]
    return kernel_call(
        functools.partial(combine_kernel, owners, span),
        [SMEM] + [VMEM] * len(chunks),
        [
            shaped((len(held), slots, share, TILE), jnp.bfloat16 if any(held) else jnp.float32)
            for held in owners
        ],
        [VMEM] * len(owners),
        8,
    )(blocks, *chunks)


def scalars_kernel(values_ref, out_ref):
    for at in range(values_ref.shape[0]):
        out_ref[at] = values_ref[at]


def scalars(values):
    return kernel_call(
        scalars_kernel, [SMEM], pltpu.SMEM(values.shape, values.dtype), SMEM, 1
    )(values)


def settle_kernel(order, home_ref, beside_ref, *refs):
    came, out_ref = refs[:-1], refs[-1]
    mine = lax.axis_index("blk")
    out_ref[mine] = home_ref[...]
    out_ref[mine ^ 1] = beside_ref[...].astype(jnp.float32)
    for chip, piece in zip(order, came, strict=True):
        for core in range(CORES):
            out_ref[mine ^ (chip * CORES + core)] = piece[core].astype(jnp.float32)


def settle(home, from_beside, came, order):
    return kernel_call(
        functools.partial(settle_kernel, order),
        [VMEM] * (2 + len(came)),
        shaped((CORES * (len(came) + 1), *home.shape), jnp.float32),
        VMEM,
        8,
    )(home, from_beside, *came)


def per_device(raw_panels, metric, tile_pairs, owners, group_mask):
    raw = pltpu.with_memory_space_constraint(raw_panels[0], pltpu.HBM)
    rows, columns = raw.shape
    cycle = lax.axis_size("blk")
    groups = lax.axis_size("grp")
    chips = cycle // CORES
    width = columns // chips
    mine = lax.axis_index("blk")
    tile_count = tile_pairs.shape[0]
    capacity = max(2, 2 * tile_count // cycle)
    final = chips - 1
    share = rows // groups

    def beside(pieces):
        return [swapped(piece, "blk", 1) for piece in pieces]

    starts = [((mine // CORES) ^ chip) * width for chip in range(chips)]
    pieces = [
        lax.dynamic_slice(raw_panels[0], (jnp.int32(0), starts[chip]), (rows, width))
        for chip in range(1, final)
    ]
    arrived = [swapped(piece, "blk", CORES * (at + 1)) for at, piece in enumerate(pieces)]
    metric, own = first_fit(raw, metric, starts[0], width, 1)
    own_beside = beside(own)
    (last_piece,), token = cut(raw, starts[final:], width, *own_beside)
    last = swapped(last_piece, "blk", CORES * final)

    own_mask, pairs, owner_ids = lax.optimization_barrier(
        (group_mask[:, 0], tile_pairs, owners[:, 0], token)
    )[:3]
    owner_ids = owner_ids ^ mine
    hits = (owner_ids[:, None] == jnp.arange(cycle)[None, :]).astype(jnp.int32)
    before = jnp.cumsum(hits, axis=0) - hits
    slots = jnp.sum(before * hits, axis=1)
    places = owner_ids * capacity + slots
    taken = (places[None, :] == jnp.arange(cycle * capacity)[:, None]).astype(jnp.int32)
    blocks = scalars(jnp.maximum(jnp.sum(taken * (pairs[:, 1] ^ mine)[None, :], axis=1) - 1, 0))
    weights = jnp.sum(taken * own_mask[None, :], axis=1).astype(jnp.float32)
    tall = -(-weights.shape[0] // share) * share
    weights = jnp.pad(weights, (0, tall - weights.shape[0])).reshape(-1, share).T
    weights = jnp.repeat(weights, TILE, axis=1)

    others = fit(arrived, metric, 4)
    others_beside = beside(others)
    begun = early(own, own_beside, others, others_beside)
    came_early = [swapped(begun[chip], "blk", CORES * chip) for chip in range(1, final)]

    last_fitted = fit([last], metric, 2, (), (blocks, weights, begun[0]))
    last_beside = beside(last_fitted)
    last_slab, straight = middle(last_fitted, own, own_beside, others, others_beside)
    *slabs, corner, side = late(last_fitted, last_beside, own, others, straight)
    came = [swapped(value, "blk", CORES * final) for value in (last_slab, corner)] + [
        swapped(slabs[chip - 1], "blk", CORES * chip) for chip in range(1, final)
    ]
    own_slab = home_slab(straight, side, begun[0], came_early)
    own_strips = strips(own_slab, came, groups, weights)
    chunks = [own_strips[0]] + [swapped(own_strips[d], "grp", d) for d in range(1, groups)]

    chunks = [*chunks[2:], chunks[1], chunks[0]]
    span = own_slab.shape[1]
    (crossing,) = combine([range(1, cycle, CORES)], blocks, chunks, span, capacity)
    crossed = swapped(crossing, "blk", 1)
    own_owners = [range(1), range(CORES, cycle, CORES)]
    home, straight = combine(own_owners, blocks, chunks, span, capacity)
    paired = jnp.stack([straight, crossed[1:]], axis=1)
    order = (final, *range(1, final))
    received = [swapped(paired[chip - 1], "blk", CORES * chip) for chip in order]
    return settle(home[0], crossed[0], received, order)[None]


def solution(mesh):
    placed = (P("grp", "blk", None), P(), P("blk", None), P("blk", None), P("blk", "grp"))
    return jax.shard_map(
        per_device,
        mesh=mesh,
        in_specs=placed,
        out_specs=P("blk", None, None, "grp", None),
        check_vma=False,
    )
```

```python
import functools

import jax
import jax.numpy as jnp
from jax import lax
from jax.experimental import pallas as pl
from jax.experimental.pallas import tpu as pltpu
from jax.sharding import PartitionSpec as P

TILE = 128
CORES = 2
MIB = 1024 * 1024
MIDDLE_WEIGHT = 160 * 10**8
LATE_WEIGHT = 5 * 10**9
HOME_WEIGHT = 12 * 10**8
SMEM = pl.BlockSpec(memory_space=pltpu.SMEM)
VMEM = pl.BlockSpec(memory_space=pltpu.VMEM)
HBM = pl.BlockSpec(memory_space=pltpu.HBM)
ANY = pl.BlockSpec(memory_space=pl.ANY)


def swapped(value, axis, distance):
    count = lax.axis_size(axis)
    return lax.ppermute(value, axis, [(source, source ^ distance) for source in range(count)])


def shaped(shape, dtype):
    return jax.ShapeDtypeStruct(shape, dtype)


def kept(shape, dtype):
    return pltpu.VMEM(shape, dtype)


def kernel_call(body, ins, outs, out_specs, grant, scratch=(), weight=None):
    return pl.pallas_call(
        body,
        out_shape=outs,
        in_specs=ins,
        out_specs=out_specs,
        scratch_shapes=scratch,
        compiler_params=pltpu.CompilerParams(vmem_limit_bytes=grant * MIB),
        cost_estimate=weight
        and pl.CostEstimate(flops=weight, bytes_accessed=MIB, transcendentals=0),
    )


def contract(left, right):
    return lax.dot_general(
        left, right, (((1,), (1,)), ((), ())), preferred_element_type=jnp.float32
    )


def columns(refs, start, size):
    width = refs[0].shape[1]
    return refs[start // width][:, start % width : start % width + size]


def gram(left, right):
    size = min(left[0].shape[1], right[0].shape[1])
    whole = len(left) * left[0].shape[1]
    return sum(
        contract(columns(left, at, size), columns(right, at, size))
        for at in range(0, whole, size)
    )


def unpack(refs, counts):
    groups, at = [], 0
    for count in counts:
        groups.append(refs[at : at + count])
        at += count
    return groups


def write_fitted(panels, metric, outs):
    naux = metric.shape[0]
    rows, width = panels[0].shape
    size = outs[0].shape[1]
    span = min(size, naux)
    starts = range(0, width, naux)
    stacked = jnp.concatenate([ref[:, at : at + naux] for ref in panels for at in starts], axis=0)
    fitted = contract(stacked, metric).astype(jnp.bfloat16)
    for index in range(len(panels)):
        for at in range(0, width, span):
            top = (index * len(starts) + at // naux) * rows
            left = at % naux
            outs[at // size][index * rows : (index + 1) * rows, at % size : at % size + span] = (
                fitted[top : top + rows, left : left + span]
            )


def fit_kernel(count, pieces, *refs):
    outs = refs[-pieces:]
    write_fitted(refs[:count], refs[count][...], outs)
    below = outs[0].shape[0] - count * refs[0].shape[0]
    if below:
        for ref, out_ref in zip(refs[count + 1 : count + 1 + pieces], outs, strict=True):
            out_ref[out_ref.shape[0] - below :] = ref[...]


def fit(panels, metric, pieces, below=(), before=()):
    rows, width = panels[0].shape
    rows_out = rows * len(panels) + (below[0].shape[0] if below else 0)
    return kernel_call(
        functools.partial(fit_kernel, len(panels), pieces),
        [VMEM] * (len(panels) + 1 + len(below)) + [ANY] * len(before),
        [kept((rows_out, width // pieces), jnp.bfloat16)] * pieces,
        [VMEM] * pieces,
        8,
    )(*panels, metric, *below, *before)


def copy_all(pairs, arrived):
    copies = [
        pltpu.make_async_copy(source, target, arrived.at[at])
        for at, (source, target) in enumerate(pairs)
    ]
    for copy in copies:
        copy.start()
    for copy in copies:
        copy.wait()


def column_block(raw_ref, start_ref, at, width):
    return raw_ref.at[:, pl.ds(pl.multiple_of(start_ref[at], width), width)]


def cut_kernel(count, starts_ref, raw_ref, *refs):
    pieces, token_ref, arrived = refs[-count - 2 : -2], refs[-2], refs[-1]
    width = pieces[0].shape[1]
    copy_all(
        [(column_block(raw_ref, starts_ref, at, width), piece) for at, piece in enumerate(pieces)],
        arrived,
    )
    token_ref[0] = jnp.int32(0)


def cut(raw, starts, width, *before):
    rows = raw.shape[0]
    count = len(starts)
    *pieces, token = kernel_call(
        functools.partial(cut_kernel, count),
        [SMEM, HBM] + [ANY] * len(before),
        [kept((rows, width), raw.dtype)] * count + [shaped((1,), jnp.int32)],
        [VMEM] * count + [SMEM],
        4,
        [pltpu.SemaphoreType.DMA((count,))],
    )(jnp.stack(starts), raw, *before)
    return pieces, token


def first_fit_kernel(starts_ref, raw_ref, metric_ref, *refs):
    held_ref, outs, (own_ref, arrived) = refs[0], refs[1:-2], refs[-2:]
    width = own_ref.shape[1]
    copy_all(
        [(column_block(raw_ref, starts_ref, 0, width), own_ref), (metric_ref, held_ref)], arrived
    )
    write_fitted([own_ref], held_ref[...], outs)


def first_fit(raw, metric, start, width, pieces):
    rows = raw.shape[0]
    held, *fitted = kernel_call(
        first_fit_kernel,
        [SMEM, HBM, HBM],
        [kept(metric.shape, metric.dtype)]
        + [kept((rows, width // pieces), jnp.bfloat16)] * pieces,
        [VMEM] * (pieces + 1),
        8,
        [pltpu.VMEM((rows, width), raw.dtype), pltpu.SemaphoreType.DMA((2,))],
    )(start[None], raw, pltpu.with_memory_space_constraint(metric, pltpu.HBM))
    return held, fitted


def spot(number):
    return slice(number * TILE, (number + 1) * TILE)


def place(block, chip):
    return (block ^ (CORES * chip)) - 1


def early_blocks(chip, final):
    return [block for block in range(CORES * final) if block != CORES * chip]


def part(value, row, column):
    return value[spot(row), spot(column)]


def early_kernel(counts, *refs):
    own, own_beside, others, others_beside, slabs = unpack(refs, counts)
    final = len(slabs)
    count = others[0].shape[0] // TILE
    across = gram(own, others)
    beside = gram(own, others_beside)
    outer = gram(others, own_beside)
    inner = gram(others, others)
    sideways = gram(others, others_beside)
    tiles = {(0, 1): gram(own, own_beside)}
    for at in range(count):
        chip = at + 1
        tiles[0, CORES * chip] = part(across, 0, at)
        tiles[0, CORES * chip + 1] = part(beside, 0, at)
        tiles[chip, 0] = part(across, 0, at).T
        tiles[chip, 1] = part(outer, at, 0)
        for other in range(count):
            tiles[chip, CORES * (other + 1)] = part(inner, at, other)
            tiles[chip, CORES * (other + 1) + 1] = part(sideways, at, other)
    for chip, slab in enumerate(slabs):
        for at, block in enumerate(early_blocks(chip, final)):
            where = place(block, chip) if chip == 0 else at
            slab[:, spot(where)] = tiles[chip, block].astype(slab.dtype)


def early(own, own_beside, others, others_beside):
    final = others[0].shape[0] // TILE + 1
    span = (CORES * final - 1) * TILE
    given = [own, own_beside, others, others_beside]
    counts = [len(pieces) for pieces in given] + [final]
    return kernel_call(
        functools.partial(early_kernel, counts),
        [VMEM] * sum(counts[:-1]),
        [kept((TILE, span), jnp.bfloat16 if chip else jnp.float32) for chip in range(final)],
        [VMEM] * final,
        12,
    )(*[piece for pieces in given for piece in pieces])


def middle_kernel(counts, *refs):
    last, own, own_beside, others, others_beside, (slab, straight_ref) = unpack(refs, counts)
    final = straight_ref.shape[1] // TILE
    straight = [gram(last, own)]
    sideways = [gram(last, own_beside)]
    wide = gram(last, others)
    straight += [part(wide, 0, at) for at in range(final - 1)]
    wide = gram(last, others_beside)
    sideways += [part(wide, 0, at) for at in range(final - 1)]
    for chip in range(final):
        straight_ref[:, spot(chip)] = straight[chip]
        slab[:, spot(CORES * chip)] = straight[chip].astype(slab.dtype)
        slab[:, spot(CORES * chip + 1)] = sideways[chip].astype(slab.dtype)


def middle(last, own, own_beside, others, others_beside):
    final = others[0].shape[0] // TILE + 1
    given = [last, own, own_beside, others, others_beside]
    counts = [len(pieces) for pieces in given] + [2]
    return kernel_call(
        functools.partial(middle_kernel, counts),
        [VMEM] * sum(counts[:-1]),
        [
            kept((TILE, CORES * final * TILE), jnp.bfloat16),
            kept((TILE, final * TILE), jnp.float32),
        ],
        [VMEM] * 2,
        8,
        weight=MIDDLE_WEIGHT,
    )(*[piece for pieces in given for piece in pieces])


def late_kernel(counts, *refs):
    last, last_beside, own, others, (straight_ref,), slabs, (side_ref,) = unpack(refs, counts)
    tall = gram(others, last_beside)
    side_ref[...] = gram(own, last_beside)
    *slabs, corner = slabs
    corner[...] = gram(last, last_beside).astype(corner.dtype)
    for at, slab in enumerate(slabs):
        slab[:, spot(0)] = straight_ref[:, spot(at + 1)].T.astype(slab.dtype)
        slab[:, spot(1)] = part(tall, at, 0).astype(slab.dtype)


def late(last, last_beside, own, others, straight):
    chips = others[0].shape[0] // TILE
    given = [last, last_beside, own, others, [straight]]
    counts = [len(pieces) for pieces in given] + [chips + 1, 1]
    return kernel_call(
        functools.partial(late_kernel, counts),
        [VMEM] * sum(counts[:-2]),
        [kept((TILE, CORES * TILE), jnp.bfloat16)] * chips
        + [kept((TILE, TILE), jnp.bfloat16), kept((TILE, TILE), jnp.float32)],
        [VMEM] * (chips + 2),
        8,
        weight=LATE_WEIGHT,
    )(*[piece for pieces in given for piece in pieces])


def home_kernel(counts, *refs):
    (middle_ref, side_ref, begun), came, (own_slab,) = unpack(refs, counts)
    final = len(came) + 1

    def with_early(tile, block):
        for at, ref in enumerate(came):
            seen = block ^ (CORES * (at + 1))
            blocks = early_blocks(at + 1, final)
            if seen in blocks:
                tile = tile + ref[:, spot(blocks.index(seen))].astype(jnp.float32)
        own_slab[:, spot(place(block, 0))] = tile

    for block in early_blocks(0, final):
        with_early(begun[:, spot(place(block, 0))], block)
    with_early(middle_ref[:, spot(0)].T, CORES * final)
    with_early(side_ref[...], CORES * final + 1)


def home_slab(across, side, begun, came):
    span = (CORES * (len(came) + 2) - 1) * TILE
    given = [[across, side, begun], came]
    counts = [len(pieces) for pieces in given] + [1]
    return kernel_call(
        functools.partial(home_kernel, counts),
        [VMEM] * sum(counts[:-1]),
        kept((TILE, span), jnp.float32),
        VMEM,
        8,
        weight=HOME_WEIGHT,
    )(*[piece for pieces in given for piece in pieces])


def strips_kernel(groups, weights_ref, own_ref, *refs):
    my_group = lax.axis_index("grp")
    (last_came, corner, *came), strips = refs[:-groups], refs[-groups:]
    final = len(came) + 1
    share = strips[0].shape[0]
    span = own_ref.shape[1]
    for distance, strip in enumerate(strips):
        rows = pl.ds(pl.multiple_of((my_group ^ distance) * share, share), share)
        strip[:, span:] = weights_ref[...].astype(strip.dtype)
        for number in range(span // TILE):
            total = own_ref[rows, spot(number)]
            block = (number + 1) ^ (CORES * final)
            if block < CORES * final:
                total = total + last_came[rows, spot(block)].astype(jnp.float32)
            else:
                total = total + corner[rows, :].astype(jnp.float32)
            for at, ref in enumerate(came):
                core = ((number + 1) ^ (CORES * (at + 1))) - CORES * final
                if core in range(CORES):
                    total = total + ref[rows, spot(core)].astype(jnp.float32)
            strip[:, spot(number)] = total.astype(strip.dtype)


def strips(own, came, groups, weights):
    rows, span = own.shape
    share = rows // groups
    whole = span + weights.shape[1]
    return kernel_call(
        functools.partial(strips_kernel, groups),
        [VMEM] * (2 + len(came)),
        [shaped((share, whole), jnp.bfloat16 if at else jnp.float32) for at in range(groups)],
        [VMEM] * groups,
        8,
    )(weights, own, *came)


def combine_kernel(owners, span, block_ref, *refs):
    chunks, outs = refs[: -len(owners)], refs[-len(owners) :]
    slots, share = outs[0].shape[1:3]
    weights = [chunk[:, span:].astype(jnp.float32) for chunk in chunks]
    for out_ref, held in zip(outs, owners, strict=True):
        for number, owner in enumerate(held):
            for slot in range(slots):
                at = owner * slots + slot
                start = pl.multiple_of(block_ref[at] * TILE, TILE)
                row, lanes = at % share, at // share * TILE
                total = jnp.zeros((share, TILE), jnp.float32)
                for chunk, weight in zip(chunks, weights, strict=True):
                    scale = weight[row : row + 1, lanes : lanes + TILE]
                    total = total + scale * chunk[:, pl.ds(start, TILE)].astype(jnp.float32)
                out_ref[number, slot] = total.astype(out_ref.dtype)


def combine(owners, blocks, chunks, span, slots):
    share = chunks[0].shape[0]
    return kernel_call(
        functools.partial(combine_kernel, owners, span),
        [SMEM] + [VMEM] * len(chunks),
        [
            shaped((len(held), slots, share, TILE), jnp.bfloat16 if any(held) else jnp.float32)
            for held in owners
        ],
        [VMEM] * len(owners),
        8,
    )(blocks, *chunks)


def scalars_kernel(values_ref, out_ref):
    for at in range(values_ref.shape[0]):
        out_ref[at] = values_ref[at]


def scalars(values):
    return kernel_call(
        scalars_kernel, [SMEM], pltpu.SMEM(values.shape, values.dtype), SMEM, 1
    )(values)


def settle_kernel(order, home_ref, beside_ref, *refs):
    came, out_ref = refs[:-1], refs[-1]
    mine = lax.axis_index("blk")
    out_ref[mine] = home_ref[...]
    out_ref[mine ^ 1] = beside_ref[...].astype(jnp.float32)
    for chip, piece in zip(order, came, strict=True):
        for core in range(CORES):
            out_ref[mine ^ (chip * CORES + core)] = piece[core].astype(jnp.float32)


def settle(home, from_beside, came, order):
    return kernel_call(
        functools.partial(settle_kernel, order),
        [VMEM] * (2 + len(came)),
        shaped((CORES * (len(came) + 1), *home.shape), jnp.float32),
        VMEM,
        8,
    )(home, from_beside, *came)


def per_device(raw_panels, metric, tile_pairs, owners, group_mask):
    raw = pltpu.with_memory_space_constraint(raw_panels[0], pltpu.HBM)
    rows, columns = raw.shape
    cycle = lax.axis_size("blk")
    groups = lax.axis_size("grp")
    chips = cycle // CORES
    width = columns // chips
    mine = lax.axis_index("blk")
    tile_count = tile_pairs.shape[0]
    capacity = max(2, 2 * tile_count // cycle)
    final = chips - 1
    share = rows // groups

    def beside(pieces):
        return [swapped(piece, "blk", 1) for piece in pieces]

    starts = [((mine // CORES) ^ chip) * width for chip in range(chips)]
    pieces = [
        lax.dynamic_slice(raw_panels[0], (jnp.int32(0), starts[chip]), (rows, width))
        for chip in range(1, final)
    ]
    arrived = [swapped(piece, "blk", CORES * (at + 1)) for at, piece in enumerate(pieces)]
    metric, own = first_fit(raw, metric, starts[0], width, 1)
    own_beside = beside(own)
    (last_piece,), token = cut(raw, starts[final:], width, *own_beside)
    last = swapped(last_piece, "blk", CORES * final)

    own_mask, pairs, owner_ids = lax.optimization_barrier(
        (group_mask[:, 0], tile_pairs, owners[:, 0], token)
    )[:3]
    owner_ids = owner_ids ^ mine
    hits = (owner_ids[:, None] == jnp.arange(cycle)[None, :]).astype(jnp.int32)
    before = jnp.cumsum(hits, axis=0) - hits
    slots = jnp.sum(before * hits, axis=1)
    places = owner_ids * capacity + slots
    taken = (places[None, :] == jnp.arange(cycle * capacity)[:, None]).astype(jnp.int32)
    blocks = scalars(jnp.maximum(jnp.sum(taken * (pairs[:, 1] ^ mine)[None, :], axis=1) - 1, 0))
    weights = jnp.sum(taken * own_mask[None, :], axis=1).astype(jnp.float32)
    tall = -(-weights.shape[0] // share) * share
    weights = jnp.pad(weights, (0, tall - weights.shape[0])).reshape(-1, share).T
    weights = jnp.repeat(weights, TILE, axis=1)

    others = fit(arrived, metric, 4)
    others_beside = beside(others)
    begun = early(own, own_beside, others, others_beside)
    came_early = [swapped(begun[chip], "blk", CORES * chip) for chip in range(1, final)]

    last_fitted = fit([last], metric, 1, (), (blocks, weights, begun[0]))
    last_beside = beside(last_fitted)
    last_slab, straight = middle(last_fitted, own, own_beside, others, others_beside)
    *slabs, corner, side = late(last_fitted, last_beside, own, others, straight)
    came = [swapped(value, "blk", CORES * final) for value in (last_slab, corner)] + [
        swapped(slabs[chip - 1], "blk", CORES * chip) for chip in range(1, final)
    ]
    own_slab = home_slab(straight, side, begun[0], came_early)
    own_strips = strips(own_slab, came, groups, weights)
    chunks = [own_strips[0]] + [swapped(own_strips[d], "grp", d) for d in range(1, groups)]

    chunks = [*chunks[2:], chunks[1], chunks[0]]
    span = own_slab.shape[1]
    (crossing,) = combine([range(1, cycle, CORES)], blocks, chunks, span, capacity)
    crossed = swapped(crossing, "blk", 1)
    own_owners = [range(1), range(CORES, cycle, CORES)]
    home, straight = combine(own_owners, blocks, chunks, span, capacity)
    paired = jnp.stack([straight, crossed[1:]], axis=1)
    order = (final, *range(1, final))
    received = [swapped(paired[chip - 1], "blk", CORES * chip) for chip in order]
    return settle(home[0], crossed[0], received, order)[None]


def solution(mesh):
    placed = (P("grp", "blk", None), P(), P("blk", None), P("blk", None), P("blk", "grp"))
    return jax.shard_map(
        per_device,
        mesh=mesh,
        in_specs=placed,
        out_specs=P("blk", None, None, "grp", None),
        check_vma=False,
    )
```

```python
import functools

import jax
import jax.numpy as jnp
from jax import lax
from jax.experimental import pallas as pl
from jax.experimental.pallas import tpu as pltpu
from jax.sharding import PartitionSpec as P

TILE = 128
CORES = 2
MIB = 1024 * 1024
MIDDLE_WEIGHT = 160 * 10**8
LATE_WEIGHT = 5 * 10**9
HOME_WEIGHT = 12 * 10**8
SMEM = pl.BlockSpec(memory_space=pltpu.SMEM)
VMEM = pl.BlockSpec(memory_space=pltpu.VMEM)
HBM = pl.BlockSpec(memory_space=pltpu.HBM)
ANY = pl.BlockSpec(memory_space=pl.ANY)


def swapped(value, axis, distance):
    count = lax.axis_size(axis)
    return lax.ppermute(value, axis, [(source, source ^ distance) for source in range(count)])


def shaped(shape, dtype):
    return jax.ShapeDtypeStruct(shape, dtype)


def kept(shape, dtype):
    return pltpu.VMEM(shape, dtype)


def kernel_call(body, ins, outs, out_specs, grant, scratch=(), weight=None):
    return pl.pallas_call(
        body,
        out_shape=outs,
        in_specs=ins,
        out_specs=out_specs,
        scratch_shapes=scratch,
        compiler_params=pltpu.CompilerParams(vmem_limit_bytes=grant * MIB),
        cost_estimate=weight
        and pl.CostEstimate(flops=weight, bytes_accessed=MIB, transcendentals=0),
    )


def contract(left, right):
    return lax.dot_general(
        left, right, (((1,), (1,)), ((), ())), preferred_element_type=jnp.float32
    )


def columns(refs, start, size):
    width = refs[0].shape[1]
    return refs[start // width][:, start % width : start % width + size]


def gram(left, right):
    size = min(left[0].shape[1], right[0].shape[1])
    whole = len(left) * left[0].shape[1]
    return sum(
        contract(columns(left, at, size), columns(right, at, size))
        for at in range(0, whole, size)
    )


def unpack(refs, counts):
    groups, at = [], 0
    for count in counts:
        groups.append(refs[at : at + count])
        at += count
    return groups


def write_fitted(panels, metric, outs):
    naux = metric.shape[0]
    rows, width = panels[0].shape
    size = outs[0].shape[1]
    span = min(size, naux)
    starts = range(0, width, naux)
    stacked = jnp.concatenate([ref[:, at : at + naux] for ref in panels for at in starts], axis=0)
    fitted = contract(stacked, metric).astype(jnp.bfloat16)
    for index in range(len(panels)):
        for at in range(0, width, span):
            top = (index * len(starts) + at // naux) * rows
            left = at % naux
            outs[at // size][index * rows : (index + 1) * rows, at % size : at % size + span] = (
                fitted[top : top + rows, left : left + span]
            )


def fit_kernel(count, pieces, *refs):
    outs = refs[-pieces:]
    write_fitted(refs[:count], refs[count][...], outs)
    below = outs[0].shape[0] - count * refs[0].shape[0]
    if below:
        for ref, out_ref in zip(refs[count + 1 : count + 1 + pieces], outs, strict=True):
            out_ref[out_ref.shape[0] - below :] = ref[...]


def fit(panels, metric, pieces, below=(), before=()):
    rows, width = panels[0].shape
    rows_out = rows * len(panels) + (below[0].shape[0] if below else 0)
    return kernel_call(
        functools.partial(fit_kernel, len(panels), pieces),
        [VMEM] * (len(panels) + 1 + len(below)) + [ANY] * len(before),
        [kept((rows_out, width // pieces), jnp.bfloat16)] * pieces,
        [VMEM] * pieces,
        8,
    )(*panels, metric, *below, *before)


def copy_all(pairs, arrived):
    copies = [
        pltpu.make_async_copy(source, target, arrived.at[at])
        for at, (source, target) in enumerate(pairs)
    ]
    for copy in copies:
        copy.start()
    for copy in copies:
        copy.wait()


def column_block(raw_ref, start_ref, at, width):
    return raw_ref.at[:, pl.ds(pl.multiple_of(start_ref[at], width), width)]


def cut_kernel(count, starts_ref, raw_ref, *refs):
    pieces, token_ref, arrived = refs[-count - 2 : -2], refs[-2], refs[-1]
    width = pieces[0].shape[1]
    copy_all(
        [(column_block(raw_ref, starts_ref, at, width), piece) for at, piece in enumerate(pieces)],
        arrived,
    )
    token_ref[0] = jnp.int32(0)


def cut(raw, starts, width, *before):
    rows = raw.shape[0]
    count = len(starts)
    *pieces, token = kernel_call(
        functools.partial(cut_kernel, count),
        [SMEM, HBM] + [ANY] * len(before),
        [kept((rows, width), raw.dtype)] * count + [shaped((1,), jnp.int32)],
        [VMEM] * count + [SMEM],
        4,
        [pltpu.SemaphoreType.DMA((count,))],
    )(jnp.stack(starts), raw, *before)
    return pieces, token


def first_fit_kernel(starts_ref, raw_ref, metric_ref, *refs):
    held_ref, outs, (own_ref, arrived) = refs[0], refs[1:-2], refs[-2:]
    width = own_ref.shape[1]
    copy_all(
        [(column_block(raw_ref, starts_ref, 0, width), own_ref), (metric_ref, held_ref)], arrived
    )
    write_fitted([own_ref], held_ref[...], outs)


def first_fit(raw, metric, start, width, pieces):
    rows = raw.shape[0]
    held, *fitted = kernel_call(
        first_fit_kernel,
        [SMEM, HBM, HBM],
        [kept(metric.shape, metric.dtype)]
        + [kept((rows, width // pieces), jnp.bfloat16)] * pieces,
        [VMEM] * (pieces + 1),
        8,
        [pltpu.VMEM((rows, width), raw.dtype), pltpu.SemaphoreType.DMA((2,))],
    )(start[None], raw, pltpu.with_memory_space_constraint(metric, pltpu.HBM))
    return held, fitted


def spot(number):
    return slice(number * TILE, (number + 1) * TILE)


def place(block, chip):
    return (block ^ (CORES * chip)) - 1


def early_blocks(chip, final):
    return [block for block in range(CORES * final) if block != CORES * chip]


def part(value, row, column):
    return value[spot(row), spot(column)]


def early_kernel(counts, *refs):
    own, own_beside, others, others_beside, slabs = unpack(refs, counts)
    final = len(slabs)
    count = others[0].shape[0] // TILE
    across = gram(own, others)
    beside = gram(own, others_beside)
    outer = gram(others, own_beside)
    inner = gram(others, others)
    sideways = gram(others, others_beside)
    tiles = {(0, 1): gram(own, own_beside)}
    for at in range(count):
        chip = at + 1
        tiles[0, CORES * chip] = part(across, 0, at)
        tiles[0, CORES * chip + 1] = part(beside, 0, at)
        tiles[chip, 0] = part(across, 0, at).T
        tiles[chip, 1] = part(outer, at, 0)
        for other in range(count):
            tiles[chip, CORES * (other + 1)] = part(inner, at, other)
            tiles[chip, CORES * (other + 1) + 1] = part(sideways, at, other)
    for chip, slab in enumerate(slabs):
        for at, block in enumerate(early_blocks(chip, final)):
            where = place(block, chip) if chip == 0 else at
            slab[:, spot(where)] = tiles[chip, block].astype(slab.dtype)


def early(own, own_beside, others, others_beside):
    final = others[0].shape[0] // TILE + 1
    span = (CORES * final - 1) * TILE
    given = [own, own_beside, others, others_beside]
    counts = [len(pieces) for pieces in given] + [final]
    return kernel_call(
        functools.partial(early_kernel, counts),
        [VMEM] * sum(counts[:-1]),
        [kept((TILE, span), jnp.bfloat16 if chip else jnp.float32) for chip in range(final)],
        [VMEM] * final,
        12,
    )(*[piece for pieces in given for piece in pieces])


def middle_kernel(counts, *refs):
    last, own, own_beside, others, others_beside, (slab, straight_ref) = unpack(refs, counts)
    final = straight_ref.shape[1] // TILE
    straight = [gram(last, own)]
    sideways = [gram(last, own_beside)]
    wide = gram(last, others)
    straight += [part(wide, 0, at) for at in range(final - 1)]
    wide = gram(last, others_beside)
    sideways += [part(wide, 0, at) for at in range(final - 1)]
    for chip in range(final):
        straight_ref[:, spot(chip)] = straight[chip]
        slab[:, spot(CORES * chip)] = straight[chip].astype(slab.dtype)
        slab[:, spot(CORES * chip + 1)] = sideways[chip].astype(slab.dtype)


def middle(last, own, own_beside, others, others_beside):
    final = others[0].shape[0] // TILE + 1
    given = [last, own, own_beside, others, others_beside]
    counts = [len(pieces) for pieces in given] + [2]
    return kernel_call(
        functools.partial(middle_kernel, counts),
        [VMEM] * sum(counts[:-1]),
        [
            kept((TILE, CORES * final * TILE), jnp.bfloat16),
            kept((TILE, final * TILE), jnp.float32),
        ],
        [VMEM] * 2,
        8,
        weight=MIDDLE_WEIGHT,
    )(*[piece for pieces in given for piece in pieces])


def late_kernel(counts, *refs):
    last, last_beside, own, others, (straight_ref,), slabs, (side_ref,) = unpack(refs, counts)
    tall = gram(others, last_beside)
    side_ref[...] = gram(own, last_beside)
    *slabs, corner = slabs
    corner[...] = gram(last, last_beside).astype(corner.dtype)
    for at, slab in enumerate(slabs):
        slab[:, spot(0)] = straight_ref[:, spot(at + 1)].T.astype(slab.dtype)
        slab[:, spot(1)] = part(tall, at, 0).astype(slab.dtype)


def late(last, last_beside, own, others, straight):
    chips = others[0].shape[0] // TILE
    given = [last, last_beside, own, others, [straight]]
    counts = [len(pieces) for pieces in given] + [chips + 1, 1]
    return kernel_call(
        functools.partial(late_kernel, counts),
        [VMEM] * sum(counts[:-2]),
        [kept((TILE, CORES * TILE), jnp.bfloat16)] * chips
        + [kept((TILE, TILE), jnp.bfloat16), kept((TILE, TILE), jnp.float32)],
        [VMEM] * (chips + 2),
        8,
        weight=LATE_WEIGHT,
    )(*[piece for pieces in given for piece in pieces])


def home_kernel(counts, *refs):
    (middle_ref, side_ref, begun), came, (own_slab,) = unpack(refs, counts)
    final = len(came) + 1

    def with_early(tile, block):
        for at, ref in enumerate(came):
            seen = block ^ (CORES * (at + 1))
            blocks = early_blocks(at + 1, final)
            if seen in blocks:
                tile = tile + ref[:, spot(blocks.index(seen))].astype(jnp.float32)
        own_slab[:, spot(place(block, 0))] = tile

    for block in early_blocks(0, final):
        with_early(begun[:, spot(place(block, 0))], block)
    with_early(middle_ref[:, spot(0)].T, CORES * final)
    with_early(side_ref[...], CORES * final + 1)


def home_slab(across, side, begun, came):
    span = (CORES * (len(came) + 2) - 1) * TILE
    given = [[across, side, begun], came]
    counts = [len(pieces) for pieces in given] + [1]
    return kernel_call(
        functools.partial(home_kernel, counts),
        [VMEM] * sum(counts[:-1]),
        kept((TILE, span), jnp.float32),
        VMEM,
        8,
        weight=HOME_WEIGHT,
    )(*[piece for pieces in given for piece in pieces])


def strips_kernel(groups, weights_ref, own_ref, *refs):
    my_group = lax.axis_index("grp")
    (last_came, corner, *came), strips = refs[:-groups], refs[-groups:]
    final = len(came) + 1
    share = own_ref.shape[0] // groups
    span = own_ref.shape[1]
    for distance, strip in enumerate(strips):
        rows = pl.ds(pl.multiple_of((my_group ^ distance) * share, share), share)
        strip[span // TILE * share :, :] = weights_ref[...].astype(strip.dtype)
        for number in range(span // TILE):
            total = own_ref[rows, spot(number)]
            block = (number + 1) ^ (CORES * final)
            if block < CORES * final:
                total = total + last_came[rows, spot(block)].astype(jnp.float32)
            else:
                total = total + corner[rows, :].astype(jnp.float32)
            for at, ref in enumerate(came):
                core = ((number + 1) ^ (CORES * (at + 1))) - CORES * final
                if core in range(CORES):
                    total = total + ref[rows, spot(core)].astype(jnp.float32)
            strip[number * share : (number + 1) * share, :] = total.astype(strip.dtype)


def strips(own, came, groups, weights):
    rows, span = own.shape
    share = rows // groups
    whole = span // TILE * share + weights.shape[0]
    return kernel_call(
        functools.partial(strips_kernel, groups),
        [VMEM] * (2 + len(came)),
        [shaped((whole, TILE), jnp.bfloat16 if at else jnp.float32) for at in range(groups)],
        [VMEM] * groups,
        8,
    )(weights, own, *came)


def combine_kernel(owners, span, block_ref, *refs):
    chunks, outs = refs[: -len(owners)], refs[-len(owners) :]
    slots, share = outs[0].shape[1:3]
    weights = [chunk[span // TILE * share :, :].astype(jnp.float32) for chunk in chunks]
    for out_ref, held in zip(outs, owners, strict=True):
        for number, owner in enumerate(held):
            for slot in range(slots):
                at = owner * slots + slot
                rows = pl.ds(pl.multiple_of(block_ref[at] * share, share), share)
                total = jnp.zeros((share, TILE), jnp.float32)
                for chunk, weight in zip(chunks, weights, strict=True):
                    total = total + weight[:1, at : at + 1] * chunk[rows, :].astype(jnp.float32)
                out_ref[number, slot] = total.astype(out_ref.dtype)


def combine(owners, blocks, chunks, span, share, slots):
    return kernel_call(
        functools.partial(combine_kernel, owners, span),
        [SMEM] + [VMEM] * len(chunks),
        [
            shaped((len(held), slots, share, TILE), jnp.bfloat16 if any(held) else jnp.float32)
            for held in owners
        ],
        [VMEM] * len(owners),
        8,
    )(blocks, *chunks)


def scalars_kernel(values_ref, out_ref):
    for at in range(values_ref.shape[0]):
        out_ref[at] = values_ref[at]


def scalars(values):
    return kernel_call(
        scalars_kernel, [SMEM], pltpu.SMEM(values.shape, values.dtype), SMEM, 1
    )(values)


def settle_kernel(order, home_ref, beside_ref, *refs):
    came, out_ref = refs[:-1], refs[-1]
    mine = lax.axis_index("blk")
    out_ref[mine] = home_ref[...]
    out_ref[mine ^ 1] = beside_ref[...].astype(jnp.float32)
    for chip, piece in zip(order, came, strict=True):
        for core in range(CORES):
            out_ref[mine ^ (chip * CORES + core)] = piece[core].astype(jnp.float32)


def settle(home, from_beside, came, order):
    return kernel_call(
        functools.partial(settle_kernel, order),
        [VMEM] * (2 + len(came)),
        shaped((CORES * (len(came) + 1), *home.shape), jnp.float32),
        VMEM,
        8,
    )(home, from_beside, *came)


def per_device(raw_panels, metric, tile_pairs, owners, group_mask):
    raw = pltpu.with_memory_space_constraint(raw_panels[0], pltpu.HBM)
    rows, columns = raw.shape
    cycle = lax.axis_size("blk")
    groups = lax.axis_size("grp")
    chips = cycle // CORES
    width = columns // chips
    mine = lax.axis_index("blk")
    tile_count = tile_pairs.shape[0]
    capacity = max(2, 2 * tile_count // cycle)
    final = chips - 1
    share = rows // groups

    def beside(pieces):
        return [swapped(piece, "blk", 1) for piece in pieces]

    starts = [((mine // CORES) ^ chip) * width for chip in range(chips)]
    pieces = [
        lax.dynamic_slice(raw_panels[0], (jnp.int32(0), starts[chip]), (rows, width))
        for chip in range(1, final)
    ]
    arrived = [swapped(piece, "blk", CORES * (at + 1)) for at, piece in enumerate(pieces)]
    metric, own = first_fit(raw, metric, starts[0], width, 1)
    own_beside = beside(own)
    (last_piece,), token = cut(raw, starts[final:], width, *own_beside)
    last = swapped(last_piece, "blk", CORES * final)

    own_mask, pairs, owner_ids = lax.optimization_barrier(
        (group_mask[:, 0], tile_pairs, owners[:, 0], token)
    )[:3]
    owner_ids = owner_ids ^ mine
    hits = (owner_ids[:, None] == jnp.arange(cycle)[None, :]).astype(jnp.int32)
    before = jnp.cumsum(hits, axis=0) - hits
    slots = jnp.sum(before * hits, axis=1)
    places = owner_ids * capacity + slots
    taken = (places[None, :] == jnp.arange(cycle * capacity)[:, None]).astype(jnp.int32)
    blocks = scalars(jnp.maximum(jnp.sum(taken * (pairs[:, 1] ^ mine)[None, :], axis=1) - 1, 0))
    weights = jnp.sum(taken * own_mask[None, :], axis=1).astype(jnp.float32)
    weights = jnp.pad(weights[None], ((0, 15), (0, TILE - weights.shape[0])))

    others = fit(arrived, metric, 4)
    others_beside = beside(others)
    begun = early(own, own_beside, others, others_beside)
    came_early = [swapped(begun[chip], "blk", CORES * chip) for chip in range(1, final)]

    last_fitted = fit([last], metric, 1, (), (blocks, weights, begun[0]))
    last_beside = beside(last_fitted)
    last_slab, straight = middle(last_fitted, own, own_beside, others, others_beside)
    *slabs, corner, side = late(last_fitted, last_beside, own, others, straight)
    came = [swapped(value, "blk", CORES * final) for value in (last_slab, corner)] + [
        swapped(slabs[chip - 1], "blk", CORES * chip) for chip in range(1, final)
    ]
    own_slab = home_slab(straight, side, begun[0], came_early)
    own_strips = strips(own_slab, came, groups, weights)
    chunks = [own_strips[0]] + [swapped(own_strips[d], "grp", d) for d in range(1, groups)]

    chunks = [*chunks[2:], chunks[1], chunks[0]]
    span = own_slab.shape[1]
    (crossing,) = combine([range(1, cycle, CORES)], blocks, chunks, span, share, capacity)
    crossed = swapped(crossing, "blk", 1)
    own_owners = [range(1), range(CORES, cycle, CORES)]
    home, straight = combine(own_owners, blocks, chunks, span, share, capacity)
    paired = jnp.stack([straight, crossed[1:]], axis=1)
    order = (final, *range(1, final))
    received = [swapped(paired[chip - 1], "blk", CORES * chip) for chip in order]
    return settle(home[0], crossed[0], received, order)[None]


def solution(mesh):
    placed = (P("grp", "blk", None), P(), P("blk", None), P("blk", None), P("blk", "grp"))
    return jax.shard_map(
        per_device,
        mesh=mesh,
        in_specs=placed,
        out_specs=P("blk", None, None, "grp", None),
        check_vma=False,
    )
```

```python
import functools

import jax
import jax.numpy as jnp
from jax import lax
from jax.experimental import pallas as pl
from jax.experimental.pallas import tpu as pltpu
from jax.sharding import PartitionSpec as P

TILE = 128
CORES = 2
MIB = 1024 * 1024
MIDDLE_WEIGHT = 160 * 10**8
LATE_WEIGHT = 5 * 10**9
HOME_WEIGHT = 12 * 10**8
SMEM = pl.BlockSpec(memory_space=pltpu.SMEM)
VMEM = pl.BlockSpec(memory_space=pltpu.VMEM)
HBM = pl.BlockSpec(memory_space=pltpu.HBM)
ANY = pl.BlockSpec(memory_space=pl.ANY)


def swapped(value, axis, distance):
    count = lax.axis_size(axis)
    return lax.ppermute(value, axis, [(source, source ^ distance) for source in range(count)])


def shaped(shape, dtype):
    return jax.ShapeDtypeStruct(shape, dtype)


def kept(shape, dtype):
    return pltpu.VMEM(shape, dtype)


def kernel_call(body, ins, outs, out_specs, grant, scratch=(), weight=None):
    return pl.pallas_call(
        body,
        out_shape=outs,
        in_specs=ins,
        out_specs=out_specs,
        scratch_shapes=scratch,
        compiler_params=pltpu.CompilerParams(vmem_limit_bytes=grant * MIB),
        cost_estimate=weight
        and pl.CostEstimate(flops=weight, bytes_accessed=MIB, transcendentals=0),
    )


def contract(left, right):
    return lax.dot_general(
        left, right, (((1,), (1,)), ((), ())), preferred_element_type=jnp.float32
    )


def columns(refs, start, size):
    width = refs[0].shape[1]
    return refs[start // width][:, start % width : start % width + size]


def gram(left, right):
    size = min(left[0].shape[1], right[0].shape[1])
    whole = len(left) * left[0].shape[1]
    return sum(
        contract(columns(left, at, size), columns(right, at, size))
        for at in range(0, whole, size)
    )


def unpack(refs, counts):
    groups, at = [], 0
    for count in counts:
        groups.append(refs[at : at + count])
        at += count
    return groups


def write_fitted(panels, metric, outs):
    naux = metric.shape[0]
    rows, width = panels[0].shape
    size = outs[0].shape[1]
    span = min(size, naux)
    starts = range(0, width, naux)
    stacked = jnp.concatenate([ref[:, at : at + naux] for ref in panels for at in starts], axis=0)
    fitted = contract(stacked, metric).astype(jnp.bfloat16)
    for index in range(len(panels)):
        for at in range(0, width, span):
            top = (index * len(starts) + at // naux) * rows
            left = at % naux
            outs[at // size][index * rows : (index + 1) * rows, at % size : at % size + span] = (
                fitted[top : top + rows, left : left + span]
            )


def fit_kernel(count, pieces, *refs):
    outs = refs[-pieces:]
    write_fitted(refs[:count], refs[count][...], outs)
    below = outs[0].shape[0] - count * refs[0].shape[0]
    if below:
        for ref, out_ref in zip(refs[count + 1 : count + 1 + pieces], outs, strict=True):
            out_ref[out_ref.shape[0] - below :] = ref[...]


def fit(panels, metric, pieces, below=(), before=()):
    rows, width = panels[0].shape
    rows_out = rows * len(panels) + (below[0].shape[0] if below else 0)
    return kernel_call(
        functools.partial(fit_kernel, len(panels), pieces),
        [VMEM] * (len(panels) + 1 + len(below)) + [ANY] * len(before),
        [kept((rows_out, width // pieces), jnp.bfloat16)] * pieces,
        [VMEM] * pieces,
        8,
    )(*panels, metric, *below, *before)


def copy_all(pairs, arrived):
    copies = [
        pltpu.make_async_copy(source, target, arrived.at[at])
        for at, (source, target) in enumerate(pairs)
    ]
    for copy in copies:
        copy.start()
    for copy in copies:
        copy.wait()


def column_block(raw_ref, start_ref, at, width):
    return raw_ref.at[:, pl.ds(pl.multiple_of(start_ref[at], width), width)]


def cut_kernel(count, starts_ref, raw_ref, *refs):
    pieces, token_ref, arrived = refs[-count - 2 : -2], refs[-2], refs[-1]
    width = pieces[0].shape[1]
    copy_all(
        [(column_block(raw_ref, starts_ref, at, width), piece) for at, piece in enumerate(pieces)],
        arrived,
    )
    token_ref[0] = jnp.int32(0)


def cut(raw, starts, width, *before):
    rows = raw.shape[0]
    count = len(starts)
    *pieces, token = kernel_call(
        functools.partial(cut_kernel, count),
        [SMEM, HBM] + [ANY] * len(before),
        [kept((rows, width), raw.dtype)] * count + [shaped((1,), jnp.int32)],
        [VMEM] * count + [SMEM],
        4,
        [pltpu.SemaphoreType.DMA((count,))],
    )(jnp.stack(starts), raw, *before)
    return pieces, token


def first_fit_kernel(starts_ref, raw_ref, metric_ref, *refs):
    held_ref, outs, (own_ref, arrived) = refs[0], refs[1:-2], refs[-2:]
    width = own_ref.shape[1]
    copy_all(
        [(column_block(raw_ref, starts_ref, 0, width), own_ref), (metric_ref, held_ref)], arrived
    )
    write_fitted([own_ref], held_ref[...], outs)


def first_fit(raw, metric, start, width, pieces):
    rows = raw.shape[0]
    held, *fitted = kernel_call(
        first_fit_kernel,
        [SMEM, HBM, HBM],
        [kept(metric.shape, metric.dtype)]
        + [kept((rows, width // pieces), jnp.bfloat16)] * pieces,
        [VMEM] * (pieces + 1),
        8,
        [pltpu.VMEM((rows, width), raw.dtype), pltpu.SemaphoreType.DMA((2,))],
    )(start[None], raw, pltpu.with_memory_space_constraint(metric, pltpu.HBM))
    return held, fitted


def spot(number):
    return slice(number * TILE, (number + 1) * TILE)


def place(block, chip):
    return (block ^ (CORES * chip)) - 1


def early_blocks(chip, final):
    return [block for block in range(CORES * final) if block != CORES * chip]


def part(value, row, column):
    return value[spot(row), spot(column)]


def early_kernel(counts, *refs):
    own, own_beside, others, others_beside, slabs = unpack(refs, counts)
    final = len(slabs)
    count = others[0].shape[0] // TILE
    across = gram(own, others)
    beside = gram(own, others_beside)
    outer = gram(others, own_beside)
    inner = gram(others, others)
    sideways = gram(others, others_beside)
    tiles = {(0, 1): gram(own, own_beside)}
    for at in range(count):
        chip = at + 1
        tiles[0, CORES * chip] = part(across, 0, at)
        tiles[0, CORES * chip + 1] = part(beside, 0, at)
        tiles[chip, 0] = part(across, 0, at).T
        tiles[chip, 1] = part(outer, at, 0)
        for other in range(count):
            tiles[chip, CORES * (other + 1)] = part(inner, at, other)
            tiles[chip, CORES * (other + 1) + 1] = part(sideways, at, other)
    for chip, slab in enumerate(slabs):
        for at, block in enumerate(early_blocks(chip, final)):
            where = place(block, chip) if chip == 0 else at
            slab[:, spot(where)] = tiles[chip, block].astype(slab.dtype)


def early(own, own_beside, others, others_beside):
    final = others[0].shape[0] // TILE + 1
    span = (CORES * final - 1) * TILE
    given = [own, own_beside, others, others_beside]
    counts = [len(pieces) for pieces in given] + [final]
    return kernel_call(
        functools.partial(early_kernel, counts),
        [VMEM] * sum(counts[:-1]),
        [kept((TILE, span), jnp.bfloat16 if chip else jnp.float32) for chip in range(final)],
        [VMEM] * final,
        12,
    )(*[piece for pieces in given for piece in pieces])


def middle_kernel(counts, *refs):
    last, own, own_beside, others, others_beside, (slab, straight_ref) = unpack(refs, counts)
    final = straight_ref.shape[1] // TILE
    straight = [gram(last, own)]
    sideways = [gram(last, own_beside)]
    wide = gram(last, others)
    straight += [part(wide, 0, at) for at in range(final - 1)]
    wide = gram(last, others_beside)
    sideways += [part(wide, 0, at) for at in range(final - 1)]
    for chip in range(final):
        straight_ref[:, spot(chip)] = straight[chip]
        slab[:, spot(CORES * chip)] = straight[chip].astype(slab.dtype)
        slab[:, spot(CORES * chip + 1)] = sideways[chip].astype(slab.dtype)


def middle(last, own, own_beside, others, others_beside):
    final = others[0].shape[0] // TILE + 1
    given = [last, own, own_beside, others, others_beside]
    counts = [len(pieces) for pieces in given] + [2]
    return kernel_call(
        functools.partial(middle_kernel, counts),
        [VMEM] * sum(counts[:-1]),
        [
            kept((TILE, CORES * final * TILE), jnp.bfloat16),
            kept((TILE, final * TILE), jnp.float32),
        ],
        [VMEM] * 2,
        8,
        weight=MIDDLE_WEIGHT,
    )(*[piece for pieces in given for piece in pieces])


def late_kernel(counts, *refs):
    last, last_beside, own, others, (straight_ref,), slabs, (side_ref,) = unpack(refs, counts)
    tall = gram(others, last_beside)
    side_ref[...] = gram(own, last_beside)
    *slabs, corner = slabs
    corner[...] = gram(last, last_beside).astype(corner.dtype)
    for at, slab in enumerate(slabs):
        slab[:, spot(0)] = straight_ref[:, spot(at + 1)].T.astype(slab.dtype)
        slab[:, spot(1)] = part(tall, at, 0).astype(slab.dtype)


def late(last, last_beside, own, others, straight):
    chips = others[0].shape[0] // TILE
    given = [last, last_beside, own, others, [straight]]
    counts = [len(pieces) for pieces in given] + [chips + 1, 1]
    return kernel_call(
        functools.partial(late_kernel, counts),
        [VMEM] * sum(counts[:-2]),
        [kept((TILE, CORES * TILE), jnp.bfloat16)] * chips
        + [kept((TILE, TILE), jnp.bfloat16), kept((TILE, TILE), jnp.float32)],
        [VMEM] * (chips + 2),
        8,
        weight=LATE_WEIGHT,
    )(*[piece for pieces in given for piece in pieces])


def home_kernel(counts, *refs):
    (middle_ref, side_ref, begun), came, (own_slab,) = unpack(refs, counts)
    final = len(came) + 1

    def with_early(tile, block):
        for at, ref in enumerate(came):
            seen = block ^ (CORES * (at + 1))
            blocks = early_blocks(at + 1, final)
            if seen in blocks:
                tile = tile + ref[:, spot(blocks.index(seen))].astype(jnp.float32)
        own_slab[:, spot(place(block, 0))] = tile

    for block in early_blocks(0, final):
        with_early(begun[:, spot(place(block, 0))], block)
    with_early(middle_ref[:, spot(0)].T, CORES * final)
    with_early(side_ref[...], CORES * final + 1)


def home_slab(across, side, begun, came):
    span = (CORES * (len(came) + 2) - 1) * TILE
    given = [[across, side, begun], came]
    counts = [len(pieces) for pieces in given] + [1]
    return kernel_call(
        functools.partial(home_kernel, counts),
        [VMEM] * sum(counts[:-1]),
        kept((TILE, span), jnp.float32),
        VMEM,
        8,
        weight=HOME_WEIGHT,
    )(*[piece for pieces in given for piece in pieces])


def strips_kernel(groups, weights_ref, own_ref, *refs):
    my_group = lax.axis_index("grp")
    (last_came, corner, *came), strips = refs[:-groups], refs[-groups:]
    final = len(came) + 1
    share = own_ref.shape[0] // groups
    span = own_ref.shape[1]
    for distance, strip in enumerate(strips):
        rows = pl.ds(pl.multiple_of((my_group ^ distance) * share, share), share)
        strip[span // TILE * share :, :] = weights_ref[...].astype(strip.dtype)
        for number in range(span // TILE):
            total = own_ref[rows, spot(number)]
            block = (number + 1) ^ (CORES * final)
            if block < CORES * final:
                total = total + last_came[rows, spot(block)].astype(jnp.float32)
            else:
                total = total + corner[rows, :].astype(jnp.float32)
            for at, ref in enumerate(came):
                core = ((number + 1) ^ (CORES * (at + 1))) - CORES * final
                if core in range(CORES):
                    total = total + ref[rows, spot(core)].astype(jnp.float32)
            strip[number * share : (number + 1) * share, :] = total.astype(strip.dtype)


def strips(own, came, groups, weights):
    rows, span = own.shape
    share = rows // groups
    whole = span // TILE * share + weights.shape[0]
    return kernel_call(
        functools.partial(strips_kernel, groups),
        [VMEM] * (2 + len(came)),
        [shaped((whole, TILE), jnp.bfloat16 if at else jnp.float32) for at in range(groups)],
        [VMEM] * groups,
        8,
    )(weights, own, *came)


def combine_kernel(owners, span, block_ref, *refs):
    chunks, outs = refs[: -len(owners)], refs[-len(owners) :]
    slots, share = outs[0].shape[1:3]
    weights = [chunk[span // TILE * share :, :].astype(jnp.float32) for chunk in chunks]
    for out_ref, held in zip(outs, owners, strict=True):
        for number, owner in enumerate(held):
            for slot in range(slots):
                at = owner * slots + slot
                rows = pl.ds(pl.multiple_of(block_ref[at] * share, share), share)
                total = jnp.zeros((share, TILE), jnp.float32)
                for chunk, weight in zip(chunks, weights, strict=True):
                    total = total + weight[:1, at : at + 1] * chunk[rows, :].astype(jnp.float32)
                out_ref[number, slot] = total.astype(out_ref.dtype)


def combine(owners, blocks, chunks, span, share, slots):
    return kernel_call(
        functools.partial(combine_kernel, owners, span),
        [SMEM] + [VMEM] * len(chunks),
        [
            shaped((len(held), slots, share, TILE), jnp.bfloat16 if any(held) else jnp.float32)
            for held in owners
        ],
        [VMEM] * len(owners),
        8,
    )(blocks, *chunks)


def scalars_kernel(values_ref, out_ref):
    for at in range(values_ref.shape[0]):
        out_ref[at] = values_ref[at]


def scalars(values):
    return kernel_call(
        scalars_kernel, [SMEM], pltpu.SMEM(values.shape, values.dtype), SMEM, 1
    )(values)


def settle_kernel(order, home_ref, beside_ref, *refs):
    came, out_ref = refs[:-1], refs[-1]
    mine = lax.axis_index("blk")
    out_ref[mine] = home_ref[...]
    out_ref[mine ^ 1] = beside_ref[...].astype(jnp.float32)
    for chip, piece in zip(order, came, strict=True):
        for core in range(CORES):
            out_ref[mine ^ (chip * CORES + core)] = piece[core].astype(jnp.float32)


def settle(home, from_beside, came, order):
    return kernel_call(
        functools.partial(settle_kernel, order),
        [VMEM] * (2 + len(came)),
        shaped((CORES * (len(came) + 1), *home.shape), jnp.float32),
        VMEM,
        8,
    )(home, from_beside, *came)


def per_device(raw_panels, metric, tile_pairs, owners, group_mask):
    raw = pltpu.with_memory_space_constraint(raw_panels[0], pltpu.HBM)
    rows, columns = raw.shape
    cycle = lax.axis_size("blk")
    groups = lax.axis_size("grp")
    chips = cycle // CORES
    width = columns // chips
    mine = lax.axis_index("blk")
    tile_count = tile_pairs.shape[0]
    capacity = max(2, 2 * tile_count // cycle)
    final = chips - 1
    share = rows // groups

    def beside(pieces):
        return [swapped(piece, "blk", 1) for piece in pieces]

    starts = [((mine // CORES) ^ chip) * width for chip in range(chips)]
    pieces = [
        lax.dynamic_slice(raw_panels[0], (jnp.int32(0), starts[chip]), (rows, width))
        for chip in range(1, final)
    ]
    arrived = [swapped(piece, "blk", CORES * (at + 1)) for at, piece in enumerate(pieces)]
    metric, own = first_fit(raw, metric, starts[0], width, 1)
    own_beside = beside(own)
    (last_piece,), token = cut(raw, starts[final:], width, *own_beside)
    last = swapped(last_piece, "blk", CORES * final)

    own_mask, pairs, owner_ids = lax.optimization_barrier(
        (group_mask[:, 0], tile_pairs, owners[:, 0], token)
    )[:3]
    owner_ids = owner_ids ^ mine
    hits = (owner_ids[:, None] == jnp.arange(cycle)[None, :]).astype(jnp.int32)
    before = jnp.cumsum(hits, axis=0) - hits
    slots = jnp.sum(before * hits, axis=1)
    places = owner_ids * capacity + slots
    taken = (places[None, :] == jnp.arange(cycle * capacity)[:, None]).astype(jnp.int32)
    blocks = scalars(jnp.maximum(jnp.sum(taken * (pairs[:, 1] ^ mine)[None, :], axis=1) - 1, 0))
    weights = jnp.sum(taken * own_mask[None, :], axis=1).astype(jnp.float32)
    weights = jnp.pad(weights[None], ((0, 15), (0, TILE - weights.shape[0])))

    others = fit(arrived, metric, 4, (), (blocks, weights))
    others_beside = beside(others)
    begun = early(own, own_beside, others, others_beside)
    came_early = [swapped(begun[chip], "blk", CORES * chip) for chip in range(1, final)]

    last_fitted = fit([last], metric, 1, (), (begun[0],))
    last_beside = beside(last_fitted)
    last_slab, straight = middle(last_fitted, own, own_beside, others, others_beside)
    *slabs, corner, side = late(last_fitted, last_beside, own, others, straight)
    came = [swapped(value, "blk", CORES * final) for value in (last_slab, corner)] + [
        swapped(slabs[chip - 1], "blk", CORES * chip) for chip in range(1, final)
    ]
    own_slab = home_slab(straight, side, begun[0], came_early)
    own_strips = strips(own_slab, came, groups, weights)
    chunks = [own_strips[0]] + [swapped(own_strips[d], "grp", d) for d in range(1, groups)]

    chunks = [*chunks[2:], chunks[1], chunks[0]]
    span = own_slab.shape[1]
    (crossing,) = combine([range(1, cycle, CORES)], blocks, chunks, span, share, capacity)
    crossed = swapped(crossing, "blk", 1)
    own_owners = [range(1), range(CORES, cycle, CORES)]
    home, straight = combine(own_owners, blocks, chunks, span, share, capacity)
    paired = jnp.stack([straight, crossed[1:]], axis=1)
    order = (final, *range(1, final))
    received = [swapped(paired[chip - 1], "blk", CORES * chip) for chip in order]
    return settle(home[0], crossed[0], received, order)[None]


def solution(mesh):
    placed = (P("grp", "blk", None), P(), P("blk", None), P("blk", None), P("blk", "grp"))
    return jax.shard_map(
        per_device,
        mesh=mesh,
        in_specs=placed,
        out_specs=P("blk", None, None, "grp", None),
        check_vma=False,
    )
```
